32 devices in a mesh: dp: 16 (over z, x, core), head: 2 (over y).
Axes of the slice: x: 2, y: 2, z: 4, core: 2. Of those that a mesh axis runs over, the one named last changes fastest.
Arguments:
- hidden_in: bfloat16 [49152, 768], P('dp'), may hold values from -6 to 6
- w_query: bfloat16 [768, 768], P(None, 'head'), may hold values from -0.21875 to 0.21875
- b_query: float32 [768], P('head'), may hold values from -3 to 3
- w_key: bfloat16 [768, 768], P(None, 'head'), may hold values from -0.21875 to 0.21875
- w_value: bfloat16 [768, 768], P(None, 'head'), may hold values from -0.21875 to 0.21875
- b_value: float32 [768], P('head'), may hold values from -3 to 3
- w_out: bfloat16 [768, 768], replicated, may hold values from -2.5 to 2.5
- b_out: float32 [768], replicated, may hold values from -3 to 3
- gain_one: float32 [768], replicated, may hold values from 0.5 to 1.5
- shift_one: float32 [768], replicated, may hold values from -3 to 3
- w_up: bfloat16 [768, 3072], replicated, may hold values from -0.21875 to 0.21875
- b_up: float32 [3072], replicated, may hold values from -3 to 3
- w_down: bfloat16 [3072, 768], replicated, may hold values from -0.109375 to 0.109375
- b_down: float32 [768], replicated, may hold values from -3 to 3
- gain_two: float32 [768], replicated, may hold values from 0.5 to 1.5
- shift_two: float32 [768], replicated, may hold values from -3 to 3
- seq_length: int32 [16], P('dp'), may hold values from 1024 to 1536, as said below
- block_perm: int32 [96, 12], P('dp', 'head'), may hold values from 0 to 2, as said below
- cotangent: bfloat16 [49152, 768], P(('dp', 'head')), may hold values from -6 to 6
Outputs:
- block_out: bfloat16 [49152, 768], P(('dp', 'head'))
- input_grad: float32 [49152, 768], P(('dp', 'head'))
- grad_query: float32 [768, 768], P(None, 'head')
- grad_query_bias: float32 [768], P('head')
- grad_key: float32 [768, 768], P(None, 'head')
- grad_value: float32 [768, 768], P(None, 'head')
- grad_value_bias: float32 [768], P('head')
- grad_out: float32 [768, 768], P(None, 'head')
- grad_out_bias: float32 [768], P('head')
- grad_gain_one: float32 [768], P('head')
- grad_shift_one: float32 [768], P('head')
- grad_up: float32 [768, 3072], P(None, 'head')
- grad_up_bias: float32 [3072], P('head')
- grad_down: float32 [3072, 768], P(None, 'head')
- grad_down_bias: float32 [768], P('head')
- grad_gain_two: float32 [768], P('head')
- grad_shift_two: float32 [768], P('head')
The draws below stay inside these ranges and needn't reach their ends.
Inputs may be any that keep to these rules, and one draw needn't show every extreme that they name: `seq_length`: every sequence of one index of dp has the same length, 1024 or 1536; some index has each. `block_perm`: for each head, the entries of the blocks of one sequence are the numbers 0 to (its blocks - 1), each once.
All inputs are finite; a program needn't handle non-finite values.
Results may differ from the reference program's by a relative error of at most 0.014.
Values may be sent and summed in bfloat16 or wider, within the bound.
No kernel may reach another device: no remote copies, remote signals or barrier semaphores. Data moves between devices by JAX's collectives and lax.ppermute only.
A program may use at most 192 MiB of HBM per device.

```python
import jax
import jax.numpy as jnp
from jax import lax

D = 768
HEADS = 12
HEAD_DIM = 64
FF = 3072
BLOCK = 512
GROUP_BLOCKS = 6
TOKENS = 49152
N_DP = 16


def group_lengths(key):
    key_long, key_short, key_rest = jax.random.split(key, 3)
    blocks_each = jax.random.randint(key_rest, (N_DP,), 2, 4)
    long_group = jax.random.randint(key_long, (), 0, N_DP)
    short_group = (long_group + jax.random.randint(key_short, (), 1, N_DP)) % N_DP
    groups = jnp.arange(N_DP)
    blocks_each = jnp.where(groups == long_group, 3, jnp.where(groups == short_group, 2, blocks_each))
    return blocks_each.astype(jnp.int32)


def draw_seq_length(key, part):
    blocks_each = group_lengths(key)
    return (blocks_each * BLOCK).astype(jnp.int32)


def draw_block_perm(key, part):
    blocks_each = group_lengths(key)
    key = jax.random.fold_in(key, 7)
    drawn = jax.random.randint(key, (N_DP, GROUP_BLOCKS, HEADS), 0, 1 << 20)
    position = jnp.arange(GROUP_BLOCKS)
    per_seq = blocks_each[:, None]
    seq_index = position[None, :] // per_seq
    local_pos = position[None, :] % per_seq
    distinct = drawn * 4 + local_pos[:, :, None]
    same_seq = seq_index[:, :, None] == seq_index[:, None, :]
    lower = distinct[:, None, :, :] < distinct[:, :, None, :]
    ranks = jnp.sum(jnp.where(same_seq[..., None], lower, False), axis=2)
    return ranks.reshape(N_DP * GROUP_BLOCKS, HEADS).astype(jnp.int32)


def levels(own_key, dims, shards, smallest, top_value):
    def one(dim, parts):
        draws = jax.random.uniform(jax.random.fold_in(jax.random.fold_in(own_key, 6), dim), (parts,), jnp.float32, smallest / len(shards), top_value / len(shards))
        return jnp.repeat(jnp.exp(draws), dims[dim] // parts).reshape((-1,) + (1,) * (len(dims) - dim - 1))

    level = one(*shards[0])
    for cut in shards[1:]:
        level = level * one(*cut)
    return level


def normal_values(own_key, extent, scale, bound, cuts=(), kind=jnp.bfloat16):
    values = jax.random.normal(own_key, extent, jnp.float32) * scale
    if len(cuts) > 0:
        values = levels(own_key, extent, cuts, -0.22, 0.18) * values
    return jnp.clip(values, min=-bound, max=bound).astype(kind)


def setup_inputs(seed: int = 0) -> dict:
    key_list = jax.random.split(jax.random.key(seed), 20)
    hidden_in = normal_values(key_list[0], (TOKENS, D), 1.0, 6.0, ((0, 16),))
    w_query = normal_values(key_list[1], (D, D), D ** -0.5, 0.21875, ((1, 2),))
    b_query = normal_values(key_list[2], (D,), 0.5, 3.0, ((0, 2),), jnp.float32)
    w_key = normal_values(key_list[3], (D, D), D ** -0.5, 0.21875, ((1, 2),))
    w_value = normal_values(key_list[4], (D, D), D ** -0.5, 0.21875, ((1, 2),))
    b_value = normal_values(key_list[5], (D,), 0.5, 3.0, ((0, 2),), jnp.float32)
    w_out = normal_values(key_list[6], (D, D), (max(D // 128, 4)) ** -0.5, 2.5)
    b_out = normal_values(key_list[7], (D,), 0.5, 3.0, (), jnp.float32)
    gain_one = jnp.clip(1.0 + 0.1 * jax.random.normal(key_list[8], (D,), jnp.float32), 0.5, 1.5)
    shift_one = normal_values(key_list[9], (D,), 0.5, 3.0, (), jnp.float32)
    w_up = normal_values(key_list[10], (D, FF), D ** -0.5, 0.21875)
    b_up = normal_values(key_list[11], (FF,), 0.5, 3.0, (), jnp.float32)
    w_down = normal_values(key_list[12], (FF, D), FF ** -0.5, 0.109375)
    b_down = normal_values(key_list[13], (D,), 0.5, 3.0, (), jnp.float32)
    gain_two = jnp.clip(1.0 + 0.1 * jax.random.normal(key_list[14], (D,), jnp.float32), 0.5, 1.5)
    shift_two = normal_values(key_list[15], (D,), 0.5, 3.0, (), jnp.float32)
    seq_length = draw_seq_length(jax.random.fold_in(key_list[19], 71), 0)
    block_perm = draw_block_perm(jax.random.fold_in(key_list[19], 71), 0)
    cotangent = normal_values(key_list[18], (TOKENS, D), 1.0, 6.0, ((0, 32),))
    return {"hidden_in": hidden_in, "w_query": w_query, "b_query": b_query, "w_key": w_key, "w_value": w_value, "b_value": b_value, "w_out": w_out, "b_out": b_out, "gain_one": gain_one, "shift_one": shift_one, "w_up": w_up, "b_up": b_up, "w_down": w_down, "b_down": b_down, "gain_two": gain_two, "shift_two": shift_two, "seq_length": seq_length, "block_perm": block_perm, "cotangent": cotangent}


norm_epsilon = 1e-05

@jax.custom_vjp
def reduced_precision(v):
    return lax.optimization_barrier(v.astype(jnp.bfloat16)).astype(jnp.float32)

@jax.custom_vjp
def reduced_backward(v):
    return v

def low_keep(v):
    return (reduced_precision(v), None)

def low_pass(kept, grad):
    return (grad,)

def back_keep(v):
    return (v, None)

def back_low(kept, grad):
    return (reduced_precision(grad),)
reduced_precision.defvjp(low_keep, low_pass)
reduced_backward.defvjp(back_keep, back_low)

def matmul(left, right):
    return jnp.dot(left, right, precision=lax.Precision.HIGHEST)

def layer_norm(summed, gain, shift):
    average = lax.optimization_barrier(jnp.mean(summed, axis=-1, keepdims=True))
    centred = summed - average
    variance = lax.optimization_barrier(jnp.mean(centred * centred, axis=-1, keepdims=True))
    return centred * lax.rsqrt(variance + norm_epsilon) * gain + shift

def head_attention(inputs):
    head_query, key_head, value_head, chosen = inputs
    selected_keys = key_head[chosen]
    selected_values = value_head[chosen]
    unscaled_scores = reduced_backward(jnp.einsum('alj,axj->alx', head_query, selected_keys, precision=lax.Precision.HIGHEST))
    attention_probabilities = jax.nn.softmax(unscaled_scores * HEAD_DIM ** (-0.5), axis=-1)
    return jnp.einsum('ivo,ion->ivn', reduced_precision(attention_probabilities), selected_values, precision=lax.Precision.HIGHEST)

def by_head(matrix):
    return matrix.reshape(GROUP_BLOCKS, BLOCK, HEADS, HEAD_DIM).transpose(2, 0, 1, 3)

def group_forward(params, hidden, length, offsets):
    w_query, b_query, w_key, w_value, b_value, w_out, b_out, gain_one, shift_one, w_up, b_up, w_down, b_down, gain_two, shift_two = params
    per_seq = length // BLOCK
    position = jnp.arange(GROUP_BLOCKS, dtype=jnp.int32)
    chosen = (position // per_seq * per_seq)[:, None] + offsets % per_seq
    query_matrix = reduced_backward(reduced_precision(matmul(hidden, w_query) + b_query))
    key_rows = reduced_backward(reduced_precision(matmul(hidden, w_key)))
    value_rows = reduced_backward(reduced_precision(matmul(hidden, w_value) + b_value))
    heads_out = lax.map(jax.checkpoint(head_attention), (by_head(query_matrix), by_head(key_rows), by_head(value_rows), chosen.T))
    attended = reduced_backward(reduced_precision(heads_out.transpose(1, 2, 0, 3).reshape(GROUP_BLOCKS * BLOCK, HEADS * HEAD_DIM)))
    branch = reduced_backward(matmul(attended, w_out) + b_out)
    normed_one = layer_norm(hidden + branch, gain_one, shift_one)
    pre_act = reduced_backward(matmul(reduced_precision(normed_one), w_up) + b_up)
    acted = reduced_precision(jax.nn.gelu(pre_act, approximate=False))
    ffn_out = reduced_backward(matmul(acted, w_down) + b_down)
    return layer_norm(normed_one + ffn_out, gain_two, shift_two)

def forward(params, hidden_all, seq_length, block_perm):
    groups_in = hidden_all.reshape(N_DP, GROUP_BLOCKS * BLOCK, HEADS * HEAD_DIM)
    offsets = block_perm.reshape(N_DP, GROUP_BLOCKS, HEADS)

    def step(carry, member):
        return (carry, jax.checkpoint(group_forward)(params, member[0], member[1], member[2]))
    carry_end, outputs = lax.scan(step, jnp.zeros((), jnp.float32), (groups_in, seq_length, offsets))
    return outputs.reshape(N_DP * GROUP_BLOCKS * BLOCK, HEADS * HEAD_DIM)

def reference(hidden_in, w_query, b_query, w_key, w_value, b_value, w_out, b_out, gain_one, shift_one, w_up, b_up, w_down, b_down, gain_two, shift_two, seq_length, block_perm, cotangent):
    params = tuple((member.astype(jnp.float32) for member in (w_query, b_query, w_key, w_value, b_value, w_out, b_out, gain_one, shift_one, w_up, b_up, w_down, b_down, gain_two, shift_two)))
    block_value, pull = jax.vjp(lambda weights, inputs: forward(weights, inputs, seq_length, block_perm), params, hidden_in.astype(jnp.float32))
    grads, input_grad = pull(cotangent.astype(jnp.float32))
    return (block_value.astype(jnp.bfloat16), input_grad, grads[0], grads[1], grads[2], grads[3], grads[4], grads[5], grads[6], grads[7], grads[8], grads[9], grads[10], grads[11], grads[12], grads[13], grads[14])
```

```python
import functools
import math

import jax
import jax.numpy as jnp
from jax import lax
from jax.experimental import pallas as pl
from jax.experimental.pallas import tpu as pltpu
from jax.sharding import PartitionSpec as P

HEAD_DIM = 64
BLOCK = 512
PAIR = 2 * HEAD_DIM
EPS = 1e-5
LOG2E = math.log2(math.e)
EXP_SCALE = LOG2E / math.sqrt(HEAD_DIM)
SCALE = 1.0 / math.sqrt(HEAD_DIM)
VMEM_LIMIT = 60 * 1024 * 1024
bf16, f32 = jnp.bfloat16, jnp.float32
NT = (((1,), (1,)), ((), ()))
TN = (((0,), (0,)), ((), ()))


def dot(left, right, dims=None):
    if dims is None:
        return jnp.dot(left, right, preferred_element_type=f32)
    return lax.dot_general(left, right, dims, preferred_element_type=f32)


def params():
    return pltpu.CompilerParams(vmem_limit_bytes=VMEM_LIMIT)


def cost(flops, moved, transcendentals=0):
    return pl.CostEstimate(
        flops=int(flops), bytes_accessed=int(moved), transcendentals=int(transcendentals)
    )


def whole(shape):
    return pl.BlockSpec(shape, lambda *_: (0,) * len(shape), pipeline_mode=pl.Buffered(1))


def colsum(values):
    return jnp.sum(values, axis=0, keepdims=True)


def attend_steps(
    own, heads, info, x_ref, weight, bq_ref, bv_ref, att_ref, qaug_ref, k_ref, v_ref, q_scr
):
    step = pl.program_id(0)

    @pl.when(step <= own)
    def _():
        x = x_ref[...]
        k_ref[step] = dot(x, weight(1)).astype(bf16)
        v_ref[step] = (dot(x, weight(2)) + bv_ref[...]).astype(bf16)

        @pl.when(step < own)
        def _():
            q_scr[step] = (dot(x, weight(0)) + bq_ref[...]).astype(bf16)

    @pl.when(step > own)
    def _():
        i = step - own - 1
        lane = lax.broadcasted_iota(jnp.int32, (BLOCK, PAIR), 1)
        low = lane < HEAD_DIM
        for pair in range(heads // 2):
            cols = slice(pair * PAIR, pair * PAIR + PAIR)
            q = q_scr[i, :, cols]
            outs = []
            for a in range(2):
                c = info[own + 1 + i * heads + 2 * pair + a]
                mine = low if a == 0 else jnp.logical_not(low)
                base = HEAD_DIM if a == 0 else 0
                k = k_ref[c, :, cols]
                v = v_ref[c, :, cols]
                s = dot(jnp.where(mine, q, jnp.zeros_like(q)), k, NT)
                m = jnp.max(s, axis=1, keepdims=True)
                p = jnp.exp2((s - m) * EXP_SCALE).astype(bf16)
                o = dot(p, jnp.where(mine, v, jnp.ones_like(v)))
                total = m + jnp.log2(o) * (1.0 / EXP_SCALE)
                hi = total.astype(bf16).astype(f32)
                rest = total - hi
                mid = rest.astype(bf16).astype(f32)
                aug = jnp.where(
                    lane == base,
                    hi,
                    jnp.where(lane == base + 1, mid, jnp.where(lane == base + 2, rest - mid, 0.0)),
                )
                qaug_ref[i, 2 * pair + a] = jnp.where(mine, q, aug.astype(bf16))
                outs.append(o / pltpu.roll(o, HEAD_DIM, 1))
            att_ref[:, cols] = jnp.where(low, outs[0], outs[1]).astype(bf16)


def attend_own_kernel(own, heads, info, x, wq, wk, wv, bq, bv, att, qaug, k, v, q_scr):
    refs = (wq, wk, wv)
    attend_steps(
        own, heads, info, x, lambda n: refs[n][...], bq, bv, att, qaug, k, v, q_scr
    )


def attend_other_kernel(own, heads, info, x, near, far, bq, bv, _, att, qaug, k, v, w, q_scr):
    rows = near.shape[1]

    @pl.when(pl.program_id(0) == 0)
    def _():
        core = info[own + 1 + own * heads]
        for n in range(3):
            w[n, pl.ds(pl.multiple_of(core * rows, rows), rows), :] = near[n]
            w[n, pl.ds(pl.multiple_of((1 - core) * rows, rows), rows), :] = far[n]

    attend_steps(own, heads, info, x, lambda n: w[n], bq, bv, att, qaug, k, v, q_scr)


def attend(info, side, x, weights, bq, bv, own, att=None):
    D = x.shape[1]
    half = bq.shape[1]
    heads = half // HEAD_DIM
    last = own
    in_specs = [
        pl.BlockSpec((BLOCK, D), lambda s, n: (n[jnp.minimum(s, last)], 0)),
        *[whole(w.shape) for w in weights],
        whole((1, half)),
        whole((1, half)),
    ]
    where = own + 1 + own * heads + 1 + side
    out_specs = [
        pl.BlockSpec((BLOCK, half), lambda s, n: (jnp.maximum(s - last - 1, 0), n[where])),
        whole((own, heads, BLOCK, PAIR)),
        whole((own + 1, BLOCK, half)),
        whole((own + 1, BLOCK, half)),
    ]
    out_shape = [
        jax.ShapeDtypeStruct((own * BLOCK, 2 * half), bf16),
        jax.ShapeDtypeStruct((own, heads, BLOCK, PAIR), bf16),
        jax.ShapeDtypeStruct((own + 1, BLOCK, half), bf16),
        jax.ShapeDtypeStruct((own + 1, BLOCK, half), bf16),
    ]
    operands = [info, x, *weights, bq, bv]
    aliases = {}
    if att is None:
        body = attend_own_kernel
    else:
        body = attend_other_kernel
        in_specs.append(pl.BlockSpec(memory_space=pl.ANY))
        operands.append(att)
        aliases = {len(operands) - 1: 0}
        out_specs.append(whole((3, D, half)))
        out_shape.append(jax.ShapeDtypeStruct((3, D, half), bf16))
    pairs = own * heads
    return pl.pallas_call(
        functools.partial(body, own, heads),
        grid_spec=pltpu.PrefetchScalarGridSpec(
            num_scalar_prefetch=1,
            grid=(2 * own + 1,),
            in_specs=in_specs,
            out_specs=out_specs,
            scratch_shapes=[pltpu.VMEM((own, BLOCK, half), bf16)],
        ),
        out_shape=out_shape,
        input_output_aliases=aliases,
        compiler_params=params(),
        cost_estimate=cost(20e9 * pairs / 18, 16e6),
        name="attend_forward",
    )(*operands)


def attend_back_kernel(
    own, heads, info, qaug_ref, k_ref, v_ref, att_ref, do_ref, dq_ref, dk_ref, dv_ref, bias_ref
):
    i = pl.program_id(0)
    lane = lax.broadcasted_iota(jnp.int32, (BLOCK, PAIR), 1)
    low = lane < HEAD_DIM

    @pl.when(i == 0)
    def _():
        dk_ref[...] = jnp.zeros_like(dk_ref)
        dv_ref[...] = jnp.zeros_like(dv_ref)
        bias_ref[...] = jnp.zeros_like(bias_ref)

    for pair in range(heads // 2):
        cols = slice(pair * PAIR, pair * PAIR + PAIR)
        do = do_ref[:, cols]
        prod = do.astype(f32) * att_ref[:, cols].astype(f32)
        dqs = []
        for a in range(2):
            c = info[own + 1 + i * heads + 2 * pair + a]
            mine = low if a == 0 else jnp.logical_not(low)
            base = HEAD_DIM if a == 0 else 0
            delta = jnp.sum(jnp.where(mine, prod, 0.0), axis=1, keepdims=True)
            hi = delta.astype(bf16).astype(f32)
            aug = jnp.where(lane == base, hi, jnp.where(lane == base + 1, delta - hi, 0.0))
            doaug = jnp.where(mine, do, aug.astype(bf16))
            k = k_ref[c, :, cols]
            v = v_ref[c, :, cols]
            extra = jnp.where((lane >= base) & (lane < base + 3), -1.0, 0.0).astype(bf16)
            q = qaug_ref[i, 2 * pair + a]
            p = jnp.exp2(dot(jnp.where(mine, k, extra), q, NT) * EXP_SCALE)
            ds = (p * dot(jnp.where(mine, v, extra), doaug, NT)).astype(bf16)
            dv = dot(p.astype(bf16), do).astype(bf16)
            dk = (dot(ds, q) * SCALE).astype(bf16)
            dqs.append(dot(ds, k, TN) * SCALE)
            dk_ref[c, :, cols] = jnp.where(mine, dk, dk_ref[c, :, cols])
            dv_ref[c, :, cols] = jnp.where(mine, dv, dv_ref[c, :, cols])
            bias_ref[1:2, cols] += colsum(jnp.where(mine, dv.astype(f32), 0.0))
        dq = jnp.where(low, dqs[0], dqs[1]).astype(bf16)
        dq_ref[:, cols] = dq
        bias_ref[0:1, cols] += colsum(dq.astype(f32))


def attend_back(info, side, qaug, k, v, att, do, own):
    heads = qaug.shape[1]
    half = k.shape[2]
    where = own + 1 + own * heads + 1 + side
    kv = (own + 1, BLOCK, half)
    rows = pl.BlockSpec((BLOCK, half), lambda s, n: (s, n[where]))
    pairs = own * heads
    return pl.pallas_call(
        functools.partial(attend_back_kernel, own, heads),
        grid_spec=pltpu.PrefetchScalarGridSpec(
            num_scalar_prefetch=1,
            grid=(own,),
            in_specs=[
                pl.BlockSpec((1, heads, BLOCK, PAIR), lambda s, n: (s, 0, 0, 0))
                if False
                else whole(qaug.shape),
                whole(kv),
                whole(kv),
                rows,
                rows,
            ],
            out_specs=[
                pl.BlockSpec((BLOCK, half), lambda s, n: (s, 0)),
                whole(kv),
                whole(kv),
                whole((8, half)),
            ],
        ),
        out_shape=[
            jax.ShapeDtypeStruct((own * BLOCK, half), bf16),
            jax.ShapeDtypeStruct(kv, bf16),
            jax.ShapeDtypeStruct(kv, bf16),
            jax.ShapeDtypeStruct((8, half), f32),
        ],
        compiler_params=params(),
        cost_estimate=cost(20e9 * pairs / 18, 16e6),
        name="attend_backward",
    )(info, qaug, k, v, att, do)


def norm_terms(z):
    mean = jnp.mean(z, axis=1, keepdims=True)
    centred = z - mean
    variance = jnp.mean(centred * centred, axis=1, keepdims=True)
    inverse = lax.rsqrt(variance + EPS)
    return centred * inverse, inverse


def norm_back(incoming, normed, inverse, gain):
    scaled = incoming * gain
    first = jnp.mean(scaled, axis=1, keepdims=True)
    second = jnp.mean(scaled * normed, axis=1, keepdims=True)
    return inverse * (scaled - first - normed * second)


ERF_P = 0.3275911 * math.sqrt(0.5)
ERF_A = tuple(
    0.5 * a for a in (0.254829592, -0.284496736, 1.421413741, -1.453152027, 1.061405429)
)


def gelu_parts(v):
    e = jnp.exp2(v * v * (-0.5 * LOG2E))
    d = 1.0 + ERF_P * jnp.abs(v)
    t = pl.reciprocal(d, approx=True)
    t = t * (2.0 - d * t)
    poly = ERF_A[4]
    for a in ERF_A[3::-1]:
        poly = a + t * poly
    tail = t * poly * e
    cdf = jnp.where(v < 0, tail, 1.0 - tail)
    return v * cdf, cdf + v * e * (1.0 / math.sqrt(2 * math.pi))


def middle_kernel(
    chunk,
    info,
    att_ref,
    x_ref,
    cot_ref,
    wo_ref,
    bo_ref,
    g1_ref,
    s1_ref,
    wu_ref,
    bu_ref,
    wd_ref,
    bd_ref,
    g2_ref,
    s2_ref,
    out_ref,
    upin_ref,
    acted_ref,
    gpre_ref,
    gffn_ref,
    gbr_ref,
    gatt_ref,
    gfirst_ref,
    vec_ref,
    slope_scr,
):
    i = pl.program_id(0)
    D, ff = wu_ref.shape
    branch = dot(att_ref[...], wo_ref[...]) + bo_ref[...]
    n1, inv1 = norm_terms(x_ref[...].astype(f32) + branch)
    y1 = n1 * g1_ref[...] + s1_ref[...]
    upin = y1.astype(bf16)
    upin_ref[...] = upin
    ffn = bd_ref[...]
    for f in range(0, ff, chunk):
        cols = slice(f, f + chunk)
        value, slope = gelu_parts(dot(upin, wu_ref[:, cols]) + bu_ref[:, cols])
        act = value.astype(bf16)
        acted_ref[:, cols] = act
        slope_scr[:, cols] = slope
        ffn = ffn + dot(act, wd_ref[cols, :])
    n2, inv2 = norm_terms(y1 + ffn)
    out_ref[...] = (n2 * g2_ref[...] + s2_ref[...]).astype(bf16)
    e = cot_ref[...].astype(f32)
    gsecond = norm_back(e, n2, inv2, g2_ref[...])
    gffn = gsecond.astype(bf16)
    gffn_ref[...] = gffn

    @pl.when(i == 0)
    def _():
        vec_ref[...] = jnp.zeros_like(vec_ref)

    gnormed = gsecond
    for f in range(0, ff, chunk):
        cols = slice(f, f + chunk)
        gp = (dot(gffn, wd_ref[cols, :], NT) * slope_scr[:, cols]).astype(bf16)
        gpre_ref[:, cols] = gp
        sums = colsum(gp.astype(f32))
        for w in range(0, chunk, D):
            row = 8 + (f + w) // D
            vec_ref[row : row + 1, :] += sums[:, w : w + D]
        gnormed = gnormed + dot(gp, wu_ref[:, cols], NT)
    gfirst = norm_back(gnormed, n1, inv1, g1_ref[...])
    gfirst_ref[...] = gfirst
    gbr = gfirst.astype(bf16)
    gbr_ref[...] = gbr
    gatt_ref[...] = dot(gbr, wo_ref[...], NT).astype(bf16)
    for row, values in enumerate(
        (gbr.astype(f32), gnormed * n1, gnormed, gffn.astype(f32), e * n2, e)
    ):
        vec_ref[row : row + 1, :] += colsum(values)


def middle(info, where, att, x, cot, consts, tile=BLOCK):
    R, D = att.shape
    FF = consts[4].shape[1]
    tiles = R // tile
    row = lambda width: pl.BlockSpec((tile, width), lambda s, n: (s, 0))
    low = jax.ShapeDtypeStruct((R, D), bf16)
    wide = jax.ShapeDtypeStruct((R, FF), bf16)
    return pl.pallas_call(
        functools.partial(middle_kernel, D),
        grid_spec=pltpu.PrefetchScalarGridSpec(
            num_scalar_prefetch=1,
            grid=(tiles,),
            in_specs=[
                row(D),
                pl.BlockSpec((tile, D), lambda s, n: (s + n[where] * tiles, 0)),
                row(D),
                *[whole(c.shape) for c in consts],
            ],
            out_specs=[row(D), row(D), row(FF), row(FF), row(D), row(D), row(D), row(D)]
            + [whole((16, D))],
            scratch_shapes=[pltpu.VMEM((tile, FF), f32)],
        ),
        out_shape=[low, low, wide, wide, low, low, low, jax.ShapeDtypeStruct((R, D), f32)]
        + [jax.ShapeDtypeStruct((16, D), f32)],
        compiler_params=params(),
        cost_estimate=cost(60e9, 60e6),
        name="middle",
    )(info, att, x, cot, *consts)


def weight_kernel(flip, n_init, info, left_ref, right_ref, *refs):
    out_ref = refs[n_init]
    product = dot(left_ref[...], right_ref[...], TN)
    if flip:
        product = product.T
    for init in refs[:n_init]:
        product = product + init[...].astype(f32)
    out_ref[...] = product.astype(bf16)


def weight_grad(left, right, left_block, right_block, m, n, inits=(), flip=False, tile=None):
    K = left.shape[0]
    tile = tile or n
    steps = n // tile
    place = jnp.stack([left_block, right_block]).astype(jnp.int32)
    if flip:
        shape = (n, m)
        out_spec = pl.BlockSpec((tile, m), lambda s, p: (s, 0))
    else:
        shape = (m, n)
        out_spec = pl.BlockSpec((m, tile), lambda s, p: (0, s))
    return pl.pallas_call(
        functools.partial(weight_kernel, flip, len(inits)),
        grid_spec=pltpu.PrefetchScalarGridSpec(
            num_scalar_prefetch=1,
            grid=(steps,),
            in_specs=[
                pl.BlockSpec((K, m), lambda s, p: (0, p[0])),
                pl.BlockSpec((K, tile), lambda s, p: (0, p[1] * steps + s)),
                *[out_spec for _ in inits],
            ],
            out_specs=out_spec,
        ),
        out_shape=jax.ShapeDtypeStruct(shape, bf16),
        compiler_params=params(),
        cost_estimate=cost(3 * K * m * n, 2 * (K * m + K * n + m * n)),
        name="weight_grad",
    )(place, left, right, *inits)


def qkv_weight_kernel(own, n_init, info, x_ref, q_ref, k_ref, v_ref, *refs):
    out_ref = refs[n_init]
    half = q_ref.shape[1]
    s = pl.program_id(0)
    x = x_ref[...]

    @pl.when(s == 0)
    def _():
        out_ref[...] = jnp.zeros_like(out_ref)
        for init in refs[:n_init]:
            out_ref[...] += init[...].astype(f32)

    @pl.when(s < own)
    def _():
        out_ref[:, :half] += dot(x, q_ref[...], TN)

    out_ref[:, half : 2 * half] += dot(x, k_ref[0], TN)
    out_ref[:, 2 * half :] += dot(x, v_ref[0], TN)


def qkv_weight(info, core_block, x, dq, dk, dv, own, inits=()):
    half = dq.shape[1]
    D = x.shape[1]
    m = D // 2
    info = jnp.concatenate([info, core_block[None]])
    at = info.shape[0] - 1

    def kernel(info, x_ref, q_ref, k_ref, v_ref, *refs):
        n_init = len(inits)
        out_ref, acc = refs[n_init], refs[n_init + 1]
        qkv_weight_kernel(own, n_init, info, x_ref, q_ref, k_ref, v_ref, *refs[:n_init], acc)

        @pl.when(pl.program_id(0) == own)
        def _():
            out_ref[...] = acc[...].astype(bf16)

    return pl.pallas_call(
        kernel,
        grid_spec=pltpu.PrefetchScalarGridSpec(
            num_scalar_prefetch=1,
            grid=(own + 1,),
            in_specs=[
                pl.BlockSpec((BLOCK, m), lambda s, n: (n[s], n[at])),
                pl.BlockSpec((BLOCK, half), lambda s, n: (jnp.minimum(s, own - 1), 0)),
                pl.BlockSpec((1, BLOCK, half), lambda s, n: (s, 0, 0)),
                pl.BlockSpec((1, BLOCK, half), lambda s, n: (s, 0, 0)),
                *[whole((m, 3 * half)) for _ in inits],
            ],
            out_specs=whole((m, 3 * half)),
            scratch_shapes=[pltpu.VMEM((m, 3 * half), f32)],
        ),
        out_shape=jax.ShapeDtypeStruct((m, 3 * half), bf16),
        compiler_params=params(),
        cost_estimate=cost(3 * 2048 * m * 3 * half, 12e6),
        name="qkv_weight",
    )(info, x, dq, dk, dv, *inits)


def foreign_kernel(*refs):
    (ka, va, kb, vb, wka, wva, wb, out_ref) = refs
    total = dot(ka[0], wka[...], NT) + dot(va[0], wva[...], NT)
    total = total + dot(kb[0], wb[1], NT) + dot(vb[0], wb[2], NT)
    out_ref[...] = total.astype(bf16)


def foreign_grad(dkv, weights, other, own):
    D, half = weights[0].shape
    block = pl.BlockSpec((1, BLOCK, half), lambda s: (own, 0, 0))
    return pl.pallas_call(
        foreign_kernel,
        grid=(1,),
        in_specs=[block] * 4 + [whole((D, half))] * 2 + [whole(other.shape)],
        out_specs=pl.BlockSpec((BLOCK, D), lambda s: (0, 0)),
        out_shape=jax.ShapeDtypeStruct((BLOCK, D), bf16),
        compiler_params=params(),
        cost_estimate=cost(3 * BLOCK * D * 4 * half, 8e6),
        name="foreign_grad",
    )(*dkv, weights[1], weights[2], other)


def input_kernel(boundary, info, qa, ka, va, qb, kb, vb, wq, wk, wv, wb, first, recv, out_ref):
    total = first[...] + dot(qa[...], wq[...], NT) + dot(ka[0], wk[...], NT)
    total = total + dot(va[0], wv[...], NT) + dot(qb[...], wb[0], NT)
    total = total + dot(kb[0], wb[1], NT) + dot(vb[0], wb[2], NT)
    edge = pl.program_id(0) == info[boundary]

    @pl.when(edge)
    def _():
        out_ref[...] = total + recv[...].astype(f32)

    @pl.when(jnp.logical_not(edge))
    def _():
        out_ref[...] = total


def input_grad_of(info, boundary, mine, others, weights, other, first, recv, own):
    D, half = weights[0].shape
    row = pl.BlockSpec((BLOCK, half), lambda s, n: (s, 0))
    stacked = pl.BlockSpec((1, BLOCK, half), lambda s, n: (s, 0, 0))
    wide = pl.BlockSpec((BLOCK, D), lambda s, n: (s, 0))
    return pl.pallas_call(
        functools.partial(input_kernel, boundary),
        grid_spec=pltpu.PrefetchScalarGridSpec(
            num_scalar_prefetch=1,
            grid=(own,),
            in_specs=[row, stacked, stacked, row, stacked, stacked]
            + [whole((D, half))] * 3
            + [whole(other.shape), wide, whole((BLOCK, D))],
            out_specs=wide,
        ),
        out_shape=jax.ShapeDtypeStruct(first.shape, f32),
        compiler_params=params(),
        cost_estimate=cost(3 * own * BLOCK * D * 6 * half, 16e6),
        name="input_grad",
    )(info, *mine, *others, *weights, other, first, recv)


def flip_head(value):
    return lax.ppermute(value, "head", [(0, 1), (1, 0)])


def flip_dp(value, bit):
    size = lax.axis_size("dp")
    return lax.ppermute(value, "dp", [(i, i ^ (1 << bit)) for i in range(size)])


def sum_low(left, right):
    return (left.astype(f32) + right.astype(f32)).astype(bf16)


def bit_of(bit):
    return (lax.axis_index("dp") >> bit) & 1


def dp_bits():
    return range(1, (lax.axis_size("dp") - 1).bit_length())


def scatter_sum(part):
    for bit in dp_bits():
        rows = part.shape[0] // 2
        own = bit_of(bit)
        sent = lax.dynamic_slice_in_dim(part, (1 - own) * rows, rows, 0)
        kept = lax.dynamic_slice_in_dim(part, own * rows, rows, 0)
        part = sum_low(kept, flip_dp(sent, bit))
    return part


def join(mine, theirs, own, axis):
    first = jnp.where(own == 0, mine, theirs)
    second = jnp.where(own == 0, theirs, mine)
    return jnp.concatenate([first, second], axis=axis)


def gather_back(part, axis):
    for bit in reversed(dp_bits()):
        part = join(part, flip_dp(part, bit), bit_of(bit), 0)
    return join(part, flip_dp(part, 0), bit_of(0), axis).astype(f32)


def sum_all(value, with_head=True):
    if with_head:
        value = value + flip_head(value)
    for bit in range((lax.axis_size("dp") - 1).bit_length()):
        value = value + flip_dp(value, bit)
    return value


def body(
    hidden_in,
    w_query,
    b_query,
    w_key,
    w_value,
    b_value,
    w_out,
    b_out,
    gain_one,
    shift_one,
    w_up,
    b_up,
    w_down,
    b_down,
    gain_two,
    shift_two,
    seq_length,
    block_perm,
    cotangent,
):
    D, half = w_query.shape
    heads = half // HEAD_DIM
    blocks = hidden_in.shape[0] // BLOCK
    own = blocks // 2
    head = lax.axis_index("head")
    core = bit_of(0)

    rows = D // 2
    low_rows = [
        lax.dynamic_slice_in_dim(w, core * rows, rows, 0) for w in (w_query, w_key, w_value)
    ]
    near = flip_head(jnp.stack(low_rows))
    far = flip_dp(near, 0)
    small = flip_head(
        jnp.concatenate([b_query, b_value, block_perm.astype(f32).reshape(-1)])
    )
    other_bq, other_bv = small[:half], small[half : 2 * half]
    other_perm = small[2 * half :].astype(jnp.int32).reshape(block_perm.shape)

    per_seq = seq_length[0] // BLOCK
    first_block = head * own
    position = first_block + jnp.arange(own, dtype=jnp.int32)
    foreign = jnp.where(head == 0, own, own - 1)
    fetched = jnp.concatenate([position, foreign[None]])
    boundary_block = jnp.where(head == 0, own - 1, 0)

    def places(perm):
        mine = lax.dynamic_slice_in_dim(perm, first_block, own, 0)
        chosen = (position // per_seq * per_seq)[:, None] + mine % per_seq
        local = chosen - first_block
        local = jnp.where((local >= 0) & (local < own), local, own)
        tail = jnp.stack([core, head, 1 - head, boundary_block])
        return jnp.concatenate([fetched, local.reshape(-1), tail]).astype(jnp.int32)

    info_a, info_b = places(block_perm), places(other_perm)
    at_head = own + 1 + own * heads + 1
    at_boundary = at_head + 2

    weights = (w_query, w_key, w_value)
    vec = lambda v: v.reshape(1, -1)
    att, q_a, k_a, v_a = attend(
        info_a, 0, hidden_in, weights, vec(b_query), vec(b_value), own
    )
    att, q_b, k_b, v_b, w_b = attend(
        info_b, 1, hidden_in, (near, far), vec(other_bq), vec(other_bv), own, att
    )
    consts = (
        w_out,
        vec(b_out),
        vec(gain_one),
        vec(shift_one),
        w_up,
        vec(b_up),
        w_down,
        vec(b_down),
        vec(gain_two),
        vec(shift_two),
    )
    block_out, upin, acted, gpre, gffn, gbr, gatt, gfirst, vectors = middle(
        info_a, at_head, att, hidden_in, cotangent, consts
    )

    FF = w_up.shape[1]
    theirs, sibling = 1 - head, 1 - core

    def up(y, c, inits=()):
        return weight_grad(upin, gpre, jnp.int32(0), 2 * y + c, D, FF // 4, inits)

    def down(y, c, inits=()):
        return weight_grad(
            gffn, acted, y, c, D // 2, FF // 2, inits, flip=True, tile=FF // 4
        )

    def out(y, c, inits=()):
        return weight_grad(gbr, att, y, c, D // 2, D // 2, inits, flip=True)

    def reduce(part):
        sent = flip_dp(part(theirs, sibling), 0)
        sent = flip_head(part(theirs, core, (sent,)))
        kept = flip_dp(part(head, sibling), 0)
        kept = part(head, core, (kept,))
        return scatter_sum(sum_low(kept, sent))

    down_piece = reduce(down)
    up_piece = reduce(up)
    out_piece = reduce(out)
    vectors = sum_all(vectors)

    dq_b, dk_b, dv_b, bias_b = attend_back(info_b, 1, q_b, k_b, v_b, att, gatt, own)
    part = flip_dp(qkv_weight(info_b, sibling, hidden_in, dq_b, dk_b, dv_b, own), 0)
    part = qkv_weight(info_b, core, hidden_in, dq_b, dk_b, dv_b, own, (part,))
    from_other = flip_head(part)
    bias_other = flip_head(bias_b)

    dq_a, dk_a, dv_a, bias_a = attend_back(info_a, 0, q_a, k_a, v_a, att, gatt, own)
    received = flip_head(foreign_grad((dk_a, dv_a, dk_b, dv_b), weights, w_b, own))
    part = flip_dp(qkv_weight(info_a, sibling, hidden_in, dq_a, dk_a, dv_a, own), 0)
    part = qkv_weight(info_a, core, hidden_in, dq_a, dk_a, dv_a, own, (part, from_other))
    qkv_piece = scatter_sum(part)
    bias = sum_all(bias_a + bias_other, with_head=False)
    input_grad = input_grad_of(
        info_a,
        at_boundary,
        (dq_a, dk_a, dv_a),
        (dq_b, dk_b, dv_b),
        weights,
        w_b,
        gfirst,
        received,
        own,
    )

    grad_down = gather_back(down_piece, 0)
    grad_up = gather_back(up_piece, 1)
    grad_out = gather_back(out_piece, 0)
    grad_qkv = gather_back(qkv_piece, 0)

    def own_half(values):
        values = values.reshape(-1)
        n = values.shape[0] // 2
        return lax.dynamic_slice_in_dim(values, head * n, n, 0)

    return (
        block_out,
        input_grad,
        grad_qkv[:, :half],
        bias[0],
        grad_qkv[:, half : 2 * half],
        grad_qkv[:, 2 * half :],
        bias[1],
        grad_out,
        own_half(vectors[0]),
        own_half(vectors[1]),
        own_half(vectors[2]),
        grad_up,
        own_half(vectors[8 : 8 + FF // D]),
        grad_down,
        own_half(vectors[3]),
        own_half(vectors[4]),
        own_half(vectors[5]),
    )


def solution(mesh):
    rows = P(("dp", "head"), None)
    cols = P(None, "head")
    piece = P("head")
    return jax.shard_map(
        body,
        mesh=mesh,
        in_specs=(
            P("dp", None),
            cols,
            piece,
            cols,
            cols,
            piece,
            *[P()] * 10,
            P("dp"),
            P("dp", "head"),
            rows,
        ),
        out_specs=(
            rows,
            rows,
            cols,
            piece,
            cols,
            cols,
            piece,
            cols,
            piece,
            piece,
            piece,
            cols,
            piece,
            cols,
            piece,
            piece,
            piece,
        ),
        check_vma=False,
    )
```

```python
import functools
import math

import jax
import jax.numpy as jnp
from jax import lax
from jax.experimental import pallas as pl
from jax.experimental.pallas import tpu as pltpu
from jax.sharding import PartitionSpec as P

HEAD_DIM = 64
BLOCK = 512
PAIR = 2 * HEAD_DIM
EPS = 1e-5
SCALE = 1.0 / math.sqrt(HEAD_DIM)
VMEM_LIMIT = 60 * 1024 * 1024
bf16, f32 = jnp.bfloat16, jnp.float32
NT = (((1,), (1,)), ((), ()))
TN = (((0,), (0,)), ((), ()))
QUICK = pl.CostEstimate(flops=1000, bytes_accessed=1000, transcendentals=0)


def dot(left, right, dims=None):
    if dims is None:
        return jnp.dot(left, right, preferred_element_type=f32)
    return lax.dot_general(left, right, dims, preferred_element_type=f32)


def params():
    return pltpu.CompilerParams(vmem_limit_bytes=VMEM_LIMIT)


def whole(shape):
    return pl.BlockSpec(shape, lambda *_: (0,) * len(shape), pipeline_mode=pl.Buffered(1))


def colsum(values):
    return jnp.sum(values, axis=0, keepdims=True)


HEAD, CORE, NEXT = range(3)


def block_row(s, info, own):
    return jnp.where(s < own, info[HEAD] * own + s, jnp.where(info[HEAD] == 0, own, own - 1))


def key_place(own, info, length, perm, i, h):
    n = length[0] // BLOCK
    p = info[HEAD] * own + i
    c = p // n * n + perm[p, h] % n - info[HEAD] * own
    return jnp.where((c >= 0) & (c < own), c, own)


def attend_steps(own, info, length, perm, x_ref, w_ref, b_ref, att_ref, qaug_ref, kv_ref, q_scr):
    step = pl.program_id(0)
    half = q_scr.shape[2]
    heads = half // HEAD_DIM

    @pl.when(step <= own)
    def _():
        x = x_ref[...]
        kv = dot(x, w_ref[:, half:])
        kv_ref[step, :, :half] = kv[:, :half].astype(bf16)
        kv_ref[step, :, half:] = (kv[:, half:] + b_ref[1:2, :]).astype(bf16)

        @pl.when(step < own)
        def _():
            q = (dot(x, w_ref[:, :half]) + b_ref[0:1, :]).astype(bf16)
            q_scr[step] = (q.astype(f32) * SCALE).astype(bf16)

    @pl.when(step > own)
    def _():
        i = step - own - 1
        lane = lax.broadcasted_iota(jnp.int32, (BLOCK, PAIR), 1)
        low = lane < HEAD_DIM
        for pair in range(heads // 2):
            cols = slice(pair * PAIR, pair * PAIR + PAIR)
            vcols = slice(half + pair * PAIR, half + pair * PAIR + PAIR)
            q = q_scr[i, :, cols]
            outs = []
            for a in range(2):
                c = key_place(own, info, length, perm, i, 2 * pair + a)
                mine = low if a == 0 else jnp.logical_not(low)
                base = HEAD_DIM if a == 0 else 0
                k = kv_ref[c, :, cols]
                v = kv_ref[c, :, vcols]
                s = dot(jnp.where(mine, q, jnp.zeros_like(q)), k, NT)
                m = jnp.max(s, axis=1, keepdims=True)
                p = jnp.exp(s - m).astype(bf16)
                o = dot(p, jnp.where(mine, v, jnp.ones_like(v)))
                total = m + jnp.log(o)
                hi = total.astype(bf16).astype(f32)
                rest = total - hi
                mid = rest.astype(bf16).astype(f32)
                aug = jnp.where(
                    lane == base,
                    hi,
                    jnp.where(lane == base + 1, mid, jnp.where(lane == base + 2, rest - mid, 0.0)),
                )
                qaug_ref[i, 2 * pair + a] = jnp.where(mine, q, aug.astype(bf16))
                outs.append(o * pl.reciprocal(pltpu.roll(o, HEAD_DIM, 1), approx=True))
            att_ref[:, cols] = jnp.where(low, outs[0], outs[1]).astype(bf16)


def attend_own_kernel(own, info, length, perm, x, w, b, att, qaug, kv, q_scr):
    attend_steps(own, info, length, perm, x, w, b, att, qaug, kv, q_scr)


def attend_other_kernel(own, info, length, perm, x, near, far, b, _, att, qaug, kv, w, q_scr):
    rows = near.shape[0]

    @pl.when(pl.program_id(0) == 0)
    def _():
        core = info[CORE]
        w[pl.ds(pl.multiple_of(core * rows, rows), rows), :] = near[...]
        w[pl.ds(pl.multiple_of((1 - core) * rows, rows), rows), :] = far[...]

    attend_steps(own, info, length, perm, x, w, b, att, qaug, kv, q_scr)


def attend(scalars, side, x, weights, biases, own, att=None):
    D = x.shape[1]
    half = D // 2
    heads = half // HEAD_DIM
    in_specs = [
        pl.BlockSpec((BLOCK, D), lambda s, n, *_: (block_row(jnp.minimum(s, own), n, own), 0)),
        *[whole(w.shape) for w in weights],
        whole(biases.shape),
    ]
    column = lambda n: n[HEAD] if side == 0 else 1 - n[HEAD]
    out_specs = [
        pl.BlockSpec((BLOCK, half), lambda s, n, *_: (jnp.maximum(s - own - 1, 0), column(n))),
        whole((own, heads, BLOCK, PAIR)),
        whole((own + 1, BLOCK, 2 * half)),
    ]
    out_shape = [
        jax.ShapeDtypeStruct((own * BLOCK, D), bf16),
        jax.ShapeDtypeStruct((own, heads, BLOCK, PAIR), bf16),
        jax.ShapeDtypeStruct((own + 1, BLOCK, 2 * half), bf16),
    ]
    operands = [*scalars, x, *weights, biases]
    aliases = {}
    if att is None:
        body = attend_own_kernel
    else:
        body = attend_other_kernel
        in_specs.append(pl.BlockSpec(memory_space=pl.ANY))
        operands.append(att)
        aliases = {len(operands) - 1: 0}
        out_specs.append(whole((D, 3 * half)))
        out_shape.append(jax.ShapeDtypeStruct((D, 3 * half), bf16))
    return pl.pallas_call(
        functools.partial(body, own),
        grid_spec=pltpu.PrefetchScalarGridSpec(
            num_scalar_prefetch=3,
            grid=(2 * own + 1,),
            in_specs=in_specs,
            out_specs=out_specs,
            scratch_shapes=[pltpu.VMEM((own, BLOCK, half), bf16)],
        ),
        out_shape=out_shape,
        input_output_aliases=aliases,
        compiler_params=params(),
        cost_estimate=QUICK,
        name="attend_forward",
    )(*operands)


def attend_back_kernel(
    own,
    info,
    length,
    perm,
    qaug_ref,
    kv_ref,
    att_ref,
    do_ref,
    x_ref,
    d_ref,
    near_ref,
    left_ref,
    right_ref,
    x_scr,
):
    step = pl.program_id(0)
    heads = qaug_ref.shape[1]
    half = heads * HEAD_DIM

    @pl.when(step == 0)
    def _():
        d_ref[...] = jnp.zeros_like(d_ref)

    x_scr[pl.ds(pl.multiple_of(step * BLOCK, BLOCK), BLOCK), :] = x_ref[...]

    @pl.when(step < own)
    def _():
        lane = lax.broadcasted_iota(jnp.int32, (BLOCK, PAIR), 1)
        low = lane < HEAD_DIM
        here = pl.ds(pl.multiple_of(step * BLOCK, BLOCK), BLOCK)
        for pair in range(heads // 2):
            cols = slice(pair * PAIR, pair * PAIR + PAIR)
            kcols = slice(half + pair * PAIR, half + pair * PAIR + PAIR)
            vcols = slice(2 * half + pair * PAIR, 2 * half + pair * PAIR + PAIR)
            do = do_ref[:, cols]
            prod = do.astype(f32) * att_ref[:, cols].astype(f32)
            dqs = []
            for a in range(2):
                c = key_place(own, info, length, perm, step, 2 * pair + a)
                mine = low if a == 0 else jnp.logical_not(low)
                base = HEAD_DIM if a == 0 else 0
                delta = jnp.sum(jnp.where(mine, prod, 0.0), axis=1, keepdims=True)
                hi = delta.astype(bf16).astype(f32)
                aug = jnp.where(lane == base, hi, jnp.where(lane == base + 1, delta - hi, 0.0))
                doaug = jnp.where(mine, do, aug.astype(bf16))
                k = kv_ref[c, :, cols]
                v = kv_ref[c, :, kcols]
                extra = jnp.where((lane >= base) & (lane < base + 3), -1.0, 0.0).astype(bf16)
                q = qaug_ref[0, 2 * pair + a]
                p = jnp.exp(dot(jnp.where(mine, k, extra), q, NT))
                ds = (p * dot(jnp.where(mine, v, extra), doaug, NT)).astype(bf16)
                dv = dot(p.astype(bf16), do).astype(bf16)
                dk = dot(ds, q).astype(bf16)
                dqs.append(dot(ds, k, TN) * SCALE)
                there = pl.ds(pl.multiple_of(c * BLOCK, BLOCK), BLOCK)
                d_ref[there, kcols] = jnp.where(mine, dk, d_ref[there, kcols])
                d_ref[there, vcols] = jnp.where(mine, dv, d_ref[there, vcols])
            d_ref[here, cols] = jnp.where(low, dqs[0], dqs[1]).astype(bf16)

    @pl.when(step == own)
    def _():
        core = info[CORE]
        d = d_ref[...]
        more = near_ref.shape[0] - half
        row = lax.broadcasted_iota(jnp.int32, (more, d.shape[1]), 0)
        sums = jnp.where(row == 0, colsum(d.astype(f32)), 0.0).astype(bf16)
        width = left_ref.shape[1]
        near_ref[half:, :] = sums
        left_ref[half:, :] = sums[:, :width]
        right_ref[half:, :] = sums[:, width:]
        x = x_scr[:, pl.ds(pl.multiple_of((1 - core) * half, half), half)]
        far = dot(x, d, TN).astype(bf16)
        left_ref[:half, :] = far[:, :width]
        right_ref[:half, :] = far[:, width:]
        x = x_scr[:, pl.ds(pl.multiple_of(core * half, half), half)]
        near_ref[:half, :] = dot(x, d, TN).astype(bf16)


def attend_back(scalars, side, qaug, kv, att, do, x, own):
    heads = qaug.shape[1]
    half = heads * HEAD_DIM
    D = x.shape[1]
    column = lambda n: n[HEAD] if side == 0 else 1 - n[HEAD]
    last = own - 1
    rows = pl.BlockSpec((BLOCK, half), lambda s, n, *_: (jnp.minimum(s, last), column(n)))
    d_shape = ((own + 1) * BLOCK, 3 * half)
    w_shape = (D // 2 + 16, 3 * half)
    w_parts = [(D // 2 + 16, width) for width in (2 * half - PAIR, half + PAIR)]
    return pl.pallas_call(
        functools.partial(attend_back_kernel, own),
        grid_spec=pltpu.PrefetchScalarGridSpec(
            num_scalar_prefetch=3,
            grid=(own + 1,),
            in_specs=[
                pl.BlockSpec(
                    (1, heads, BLOCK, PAIR), lambda s, *_: (jnp.minimum(s, last), 0, 0, 0)
                ),
                whole(kv.shape),
                rows,
                rows,
                pl.BlockSpec((BLOCK, D), lambda s, n, *_: (block_row(s, n, own), 0)),
            ],
            out_specs=[whole(d_shape), whole(w_shape), *[whole(w) for w in w_parts]],
            scratch_shapes=[pltpu.VMEM(((own + 1) * BLOCK, D), bf16)],
        ),
        out_shape=[
            jax.ShapeDtypeStruct(d_shape, bf16),
            jax.ShapeDtypeStruct(w_shape, bf16),
            *[jax.ShapeDtypeStruct(w, bf16) for w in w_parts],
        ],
        compiler_params=params(),
        cost_estimate=QUICK,
        name="attend_backward",
    )(*scalars, qaug, kv, att, do, x)


def norm_terms(z):
    mean = jnp.mean(z, axis=1, keepdims=True)
    centred = z - mean
    variance = jnp.mean(centred * centred, axis=1, keepdims=True)
    inverse = lax.rsqrt(variance + EPS)
    return centred * inverse, inverse


def norm_back(incoming, normed, inverse, gain):
    scaled = incoming * gain
    first = jnp.mean(scaled, axis=1, keepdims=True)
    second = jnp.mean(scaled * normed, axis=1, keepdims=True)
    return inverse * (scaled - first - normed * second)


def gelu_parts(v):
    cdf = 0.5 + 0.5 * lax.erf(v * math.sqrt(0.5))
    return v * cdf, cdf + v * (math.sqrt(0.5 / math.pi) * jnp.exp(v * (v * -0.5)))


def start_copies(pairs, sems):
    copies = [pltpu.make_async_copy(s, d, sems.at[n]) for n, (s, d) in enumerate(pairs)]

    @pl.when(pl.program_id(0) == 0)
    def _():
        for copy in copies:
            copy.start()

    return copies


def wait_copies(copies):
    @pl.when(pl.program_id(0) == 0)
    def _():
        for copy in copies:
            copy.wait()


def add_up(acc, rows, cols, value):
    first = pl.program_id(0) == 0
    acc[rows, cols] = jnp.where(first, value, value + acc[rows, cols])


OUT_ROWS = 32


def place_piece(info, c, y, x, near_ref, far_ref, rows, cols, piece):
    number = (info[HEAD] ^ y) * 2 + (info[NEXT] ^ x)

    @pl.when(info[CORE] == c)
    def _():
        near_ref[number, rows, cols] = piece

    @pl.when(info[CORE] != c)
    def _():
        far_ref[number, rows, cols] = piece


def middle_up_kernel(
    info,
    att_ref,
    x_ref,
    cot_ref,
    c_ref,
    wo_hbm,
    wu_hbm,
    wd_hbm,
    out_ref,
    slope_ref,
    n1_ref,
    inv_ref,
    gsec_ref,
    near_ref,
    far_ref,
    vec_ref,
    wo_ref,
    wu_ref,
    wd_ref,
    act_scr,
    acc,
    sems,
):
    i = pl.program_id(0)
    D, ff = wu_ref.shape
    copies = start_copies([(wo_hbm, wo_ref), (wu_hbm, wu_ref), (wd_hbm, wd_ref)], sems)
    bo, g1, s1, bd, g2, s2 = (c_ref[r : r + 1, :] for r in range(6))
    wait_copies(copies[:1])
    branch = dot(att_ref[...], wo_ref[...]) + bo
    n1, inv1 = norm_terms(x_ref[...].astype(f32) + branch)
    n1_ref[...] = n1
    inv_ref[...] = jnp.broadcast_to(inv1, inv_ref.shape)
    y1 = n1 * g1 + s1
    upin = y1.astype(bf16)
    wait_copies(copies[1:])
    ffn = bd
    for f in range(ff // D):
        cols = slice(f * D, f * D + D)
        value, slope = gelu_parts(dot(upin, wu_ref[:, cols]) + c_ref[8 + f : 9 + f, :])
        act = value.astype(bf16)
        act_scr[:, cols] = act
        slope_ref[:, cols] = slope.astype(bf16)
        ffn = ffn + dot(act, wd_ref[cols, :])
    n2, inv2 = norm_terms(y1 + ffn)
    out_ref[...] = (n2 * g2 + s2).astype(bf16)
    e = cot_ref[...].astype(f32)
    gsec = norm_back(e, n2, inv2, g2)
    gsec_ref[...] = gsec
    gffn = gsec.astype(bf16)
    for f in range(ff // D):
        cols = slice(f * D, f * D + D)
        add_up(acc, cols, slice(None), dot(act_scr[:, cols], gffn, TN))

    @pl.when(i == 0)
    def _():
        vec_ref[...] = jnp.zeros_like(vec_ref)

    for row, values in ((3, gffn.astype(f32)), (4, e * n2), (5, e)):
        vec_ref[row : row + 1, :] += colsum(values)

    @pl.when(i == pl.num_programs(0) - 1)
    def _():
        half = D // 2
        for number in range(4):
            near_ref[number, D:, :] = jnp.zeros((16, half), bf16)
            far_ref[number, D:, :] = jnp.zeros((16, half), bf16)
        for f in range(ff // D):
            for y in range(2):
                piece = acc[f * D : f * D + D, y * half : y * half + half].astype(bf16)
                place_piece(
                    info, f // 2, y, f % 2, near_ref, far_ref, slice(0, D), slice(None), piece
                )


def middle_up(info, att, x, cot, wo, wu, wd, consts, tile=BLOCK):
    R, D = att.shape
    FF = wu.shape[1]
    tiles = R // tile
    row = lambda width: pl.BlockSpec((tile, width), lambda s, n: (s, 0))
    anywhere = pl.BlockSpec(memory_space=pl.ANY)
    sd = jax.ShapeDtypeStruct
    pieces = (4, FF // 4 + 16, D // 2)
    return pl.pallas_call(
        middle_up_kernel,
        grid_spec=pltpu.PrefetchScalarGridSpec(
            num_scalar_prefetch=1,
            grid=(tiles,),
            in_specs=[
                row(D),
                pl.BlockSpec((tile, D), lambda s, n: (s + n[HEAD] * tiles, 0)),
                row(D),
                whole(consts.shape),
                anywhere,
                anywhere,
                anywhere,
            ],
            out_specs=[row(D), row(FF), row(D), row(128), row(D)]
            + [whole(pieces), whole(pieces), whole(consts.shape)],
            scratch_shapes=[
                pltpu.VMEM(wo.shape, bf16),
                pltpu.VMEM(wu.shape, bf16),
                pltpu.VMEM(wd.shape, bf16),
                pltpu.VMEM((tile, FF), bf16),
                pltpu.VMEM((FF, D), f32),
                pltpu.SemaphoreType.DMA((3,)),
            ],
        ),
        out_shape=[
            sd((R, D), bf16),
            sd((R, FF), bf16),
            sd((R, D), f32),
            sd((R, 128), f32),
            sd((R, D), f32),
            sd(pieces, bf16),
            sd(pieces, bf16),
            sd(consts.shape, f32),
        ],
        compiler_params=params(),
        cost_estimate=QUICK,
        name="middle_up",
    )(info, att, x, cot, consts, wo, wu, wd)


def middle_down_kernel(
    info,
    att_ref,
    slope_ref,
    n1_ref,
    inv_ref,
    gsec_ref,
    vec_in_ref,
    c_ref,
    wo_hbm,
    wu_hbm,
    wd_hbm,
    gatt_ref,
    gfirst_ref,
    near_ref,
    far_ref,
    wo_ref,
    wu_ref,
    wd_ref,
    vec_ref,
    gp_scr,
    acc,
    acc_out,
    sems,
):
    i = pl.program_id(0)
    D, ff = wu_ref.shape
    copies = start_copies([(wd_hbm, wd_ref), (wu_hbm, wu_ref), (wo_hbm, wo_ref)], sems)

    @pl.when(i == 0)
    def _():
        vec_ref[...] = vec_in_ref[...]

    wait_copies(copies[:1])
    g1, s1 = c_ref[1:2, :], c_ref[2:3, :]
    n1 = n1_ref[...]
    upin = (n1 * g1 + s1).astype(bf16)
    gsec = gsec_ref[...]
    gffn = gsec.astype(bf16)
    for f in range(ff // D):
        cols = slice(f * D, f * D + D)
        gp = (dot(gffn, wd_ref[cols, :], NT) * slope_ref[:, cols].astype(f32)).astype(bf16)
        gp_scr[:, cols] = gp
        vec_ref[8 + f : 9 + f, :] += colsum(gp.astype(f32))
    wait_copies(copies[1:])
    gnormed = gsec
    for f in range(ff // D):
        cols = slice(f * D, f * D + D)
        gp = gp_scr[:, cols]
        gnormed = gnormed + dot(gp, wu_ref[:, cols], NT)
        add_up(acc, slice(None), cols, dot(upin, gp, TN))
    gfirst = norm_back(gnormed, n1, inv_ref[:, :1], g1)
    gfirst_ref[...] = gfirst
    gbr = gfirst.astype(bf16)
    gatt_ref[...] = dot(gbr, wo_ref[...], NT).astype(bf16)
    add_up(acc_out, slice(None), slice(None), dot(gbr, att_ref[...], TN))
    for row, values in enumerate((gbr.astype(f32), gnormed * n1, gnormed)):
        vec_ref[row : row + 1, :] += colsum(values)

    @pl.when(i == pl.num_programs(0) - 1)
    def _():
        half, few = D // 2, D // 32
        for f in range(ff // D):
            for x in range(2):
                piece = acc[x * half : x * half + half, f * D : f * D + D].astype(bf16)
                place_piece(
                    info, f % 2, f // 2, x, near_ref, far_ref, slice(0, half), slice(None), piece
                )
        sums = vec_ref[...].astype(bf16)
        for number in range(4):
            near_ref[number, half + 4 * OUT_ROWS :, :] = sums
            far_ref[number, half + 4 * OUT_ROWS :, :] = sums
        for c in range(2):
            for y in range(2):
                for x in range(2):
                    for q in range(4):
                        top = (8 * y + 4 * x + q) * 2 * few
                        both = acc_out[top : top + 2 * few, c * half : c * half + half]
                        both = jnp.concatenate([both[:few], both[few:]], axis=1)
                        pad = jnp.zeros((OUT_ROWS - few, D), f32)
                        both = jnp.concatenate([both, pad], axis=0).astype(bf16)
                        rows = slice(half + q * OUT_ROWS, half + q * OUT_ROWS + OUT_ROWS)
                        place_piece(info, c, y, x, near_ref, far_ref, rows, slice(None), both)


def middle_down(info, att, saved, vectors, wo, wu, wd, consts, tile=BLOCK):
    R, D = att.shape
    FF = wu.shape[1]
    row = lambda width: pl.BlockSpec((tile, width), lambda s, n: (s, 0))
    anywhere = pl.BlockSpec(memory_space=pl.ANY)
    sd = jax.ShapeDtypeStruct
    pieces = (4, D // 2 + 4 * OUT_ROWS + consts.shape[0], FF // 4)
    return pl.pallas_call(
        middle_down_kernel,
        grid_spec=pltpu.PrefetchScalarGridSpec(
            num_scalar_prefetch=1,
            grid=(R // tile,),
            in_specs=[row(D), row(FF), row(D), row(128), row(D)]
            + [whole(consts.shape)] * 2
            + [anywhere] * 3,
            out_specs=[row(D), row(D), whole(pieces), whole(pieces)],
            scratch_shapes=[
                pltpu.VMEM(wo.shape, bf16),
                pltpu.VMEM(wu.shape, bf16),
                pltpu.VMEM(wd.shape, bf16),
                pltpu.VMEM(consts.shape, f32),
                pltpu.VMEM((tile, FF), bf16),
                pltpu.VMEM((D, FF), f32),
                pltpu.VMEM((D, D), f32),
                pltpu.SemaphoreType.DMA((3,)),
            ],
        ),
        out_shape=[
            sd((R, D), bf16),
            sd((R, D), f32),
            sd(pieces, bf16),
            sd(pieces, bf16),
        ],
        compiler_params=params(),
        cost_estimate=QUICK,
        name="middle_down",
    )(info, att, *saved, vectors, consts, wo, wu, wd)


def input_kernel(own, info, da, db, wa, wb, first, out_ref, next_ref):
    total = dot(da[...], wa[...], NT) + dot(db[...], wb[...], NT)

    @pl.when(pl.program_id(0) == 0)
    def _():
        next_ref[...] = total.astype(bf16)

    @pl.when(pl.program_id(0) > 0)
    def _():
        out_ref[...] = total + first[...]


def input_call(info, da, db, wa, wb, first, own):
    D, width = wa.shape
    row = pl.BlockSpec((BLOCK, width), lambda s, n: (jnp.where(s == 0, own, s - 1), 0))
    wide = pl.BlockSpec((BLOCK, D), lambda s, n: (jnp.maximum(s - 1, 0), 0))
    return pl.pallas_call(
        functools.partial(input_kernel, own),
        grid_spec=pltpu.PrefetchScalarGridSpec(
            num_scalar_prefetch=1,
            grid=(own + 1,),
            in_specs=[row, row, whole((D, width)), whole((D, width)), wide],
            out_specs=[wide, whole((BLOCK, D))],
        ),
        out_shape=[
            jax.ShapeDtypeStruct(first.shape, f32),
            jax.ShapeDtypeStruct((BLOCK, D), bf16),
        ],
        compiler_params=params(),
        cost_estimate=QUICK,
        name="input_grad",
    )(info, da, db, wa, wb, first)


def edge_kernel(info, recv, rest, out_ref):
    out_ref[...] = rest[...] + recv[...].astype(f32)


def edge_call(info, recv, rest, own):
    D = rest.shape[1]
    edge = pl.BlockSpec((BLOCK // 4, D), lambda s, n: (s + 4 * jnp.where(n[HEAD] == 0, own - 1, 0), 0))
    return pl.pallas_call(
        edge_kernel,
        grid_spec=pltpu.PrefetchScalarGridSpec(
            num_scalar_prefetch=1,
            grid=(4,),
            in_specs=[pl.BlockSpec((BLOCK // 4, D), lambda s, n: (s, 0)), edge],
            out_specs=edge,
        ),
        out_shape=jax.ShapeDtypeStruct(rest.shape, f32),
        input_output_aliases={2: 0},
        compiler_params=params(),
        cost_estimate=QUICK,
        name="edge_block",
    )(info, recv, rest)


def finish_up_kernel(info, vec_in_ref, parts, *refs):
    up_ref, out_ref, sums_ref, *vec_refs, scr = refs
    width = parts.shape[2]
    half, few = width // 2, width // 32
    count = parts.shape[0] // 4
    rows, size = half // count, parts.shape[1]
    for c in range(2):
        for x in range(2):
            for q in range(count):
                piece = parts[(2 * c + x) * count + q].astype(f32)
                up_ref[
                    x * half + q * rows : x * half + q * rows + rows, c * width : c * width + width
                ] = piece[:rows]
                for n in range(2):
                    top = x * (half // 2) + (2 * q + n) * few
                    scr[top : top + few, c * half : c * half + half] = piece[
                        rows : rows + few, n * half : n * half + half
                    ]
    out_ref[...] = scr[...].T
    vectors = vec_in_ref[...].astype(f32)
    mine = jnp.where(info[HEAD] == 0, vectors[:, :half], vectors[:, half:])
    for row, ref in enumerate(vec_refs):
        ref[...] = mine[row]
    chunks = sums_ref.shape[0] // width
    for n in range(chunks):
        both = jnp.where(info[HEAD] == 0, vectors[8 + n], vectors[8 + chunks + n])
        sums_ref[n * width : n * width + width] = both


def finish_up(info, vectors, parts):
    width = parts.shape[2]
    outs = [
        ((width, 2 * width), f32),
        ((width, width // 2), f32),
        ((2 * width,), f32),
        *[((width // 2,), f32)] * 6,
    ]
    scratch = [pltpu.VMEM((width // 2, width), f32)]
    return small_call(finish_up_kernel, "finish_up", outs, [info], [vectors, parts], scratch)


def small_call(kernel, name, outs, scalars, arrays, scratch=()):
    vmem = pl.BlockSpec(memory_space=pltpu.VMEM)
    smem = pl.BlockSpec(memory_space=pltpu.SMEM)
    return pl.pallas_call(
        kernel,
        in_specs=[smem] * len(scalars) + [vmem] * len(arrays),
        out_shape=[jax.ShapeDtypeStruct(shape, kind) for shape, kind in outs],
        scratch_shapes=list(scratch),
        compiler_params=params(),
        cost_estimate=QUICK,
        name=name,
    )(*scalars, *arrays)


def quarters_kernel(sections, at, place, *refs):
    terms, outs = refs[:-4], refs[-4:]
    for n, out in enumerate(outs):
        done = 0
        parts = [(start + (place[at] ^ n) * (rows // 4), rows // 4) for start, rows in sections]
        for top, rows in parts + [(sum(sections[-1]), 16)]:
            if not isinstance(top, int):
                top = pl.multiple_of(top, 16)
            values = [term[pl.ds(top, rows), :].astype(f32) for term in terms]
            if values[-1].shape[1] < out.shape[1]:
                values[-2:] = [jnp.concatenate(values[-2:], axis=1)]
            out[done : done + rows, :] = sum(values).astype(out.dtype)
            done += rows


def quarters(sections, at, place, terms):
    rows, width = sum(rows // 4 for _, rows in sections) + 16, terms[0].shape[1]
    outs = [((rows, width), f32)] + [((rows, width), bf16)] * 3
    kernel = functools.partial(quarters_kernel, sections, at)
    return small_call(kernel, "quarters", outs, [place], terms)


def join_cores_kernel(near, left, right, out):
    far = jnp.concatenate([left[...].astype(f32), right[...].astype(f32)], axis=1)
    out[...] = (near[...].astype(f32) + far).astype(bf16)


def join_cores(near, left, right):
    outs = [(near.shape, bf16)]
    return small_call(join_cores_kernel, "join_cores", outs, [], [near, left, right])[0]


def settle_up_kernel(*refs):
    terms, (part, vectors) = refs[:-2], refs[-2:]
    rows = part.shape[0]
    part[...] = sum(term[:rows, :].astype(f32) for term in terms).astype(bf16)
    vectors[...] = sum(term[rows:, :].astype(f32) for term in terms)


def settle_up(terms):
    rows, width = terms[0].shape
    outs = [((rows - 16, width), bf16), ((16, width), f32)]
    return small_call(settle_up_kernel, "settle_up", outs, [], terms)


def halves_kernel(place, *refs):
    terms, (kept, sent, scr) = refs[:4], refs[4:]
    few = kept.shape[0] - 16
    scr[...] = sum(term[...].astype(f32) for term in terms)
    for out, which in ((kept, place[1]), (sent, 1 - place[1])):
        out[:few, :] = scr[pl.ds(pl.multiple_of(which * few, 16), few), :].astype(out.dtype)
        out[few:, :] = scr[2 * few :, :].astype(out.dtype)


def halves(place, terms):
    rows, width = terms[0].shape
    shape = ((rows - 16) // 2 + 16, width)
    scratch = [pltpu.VMEM((rows, width), f32)]
    return small_call(
        halves_kernel, "halves", [(shape, f32), (shape, bf16)], [place], terms, scratch
    )


def settle_kernel(kept, got, part, q_sum, v_sum):
    few, width = part.shape
    half = width // 3
    total = kept[...] + got[...].astype(f32)
    part[...] = total[:few].astype(bf16)
    q_sum[...] = total[few, :half]
    v_sum[...] = total[few, 2 * half :]


def settle(kept, got):
    rows, width = kept.shape
    outs = [((rows - 16, width), bf16), ((width // 3,), f32), ((width // 3,), f32)]
    return small_call(settle_kernel, "settle", outs, [], [kept, got])


def finish_qkv_kernel(info, place, *refs):
    pieces, outs = refs[:8], refs[8:]
    rows = pieces[0].shape[0]
    half = outs[0].shape[1]
    for n, ref in enumerate(pieces):
        core = info[CORE] ^ (n // 4)
        top = pl.multiple_of((4 * core + (place[0] ^ (n % 4))) * rows, 8)
        piece = ref[...].astype(f32)
        for m, out in enumerate(outs):
            out[pl.ds(top, rows), :] = piece[:, m * half : m * half + half]


def finish_qkv(info, place, pieces):
    rows, width = pieces[0].shape
    outs = [((8 * rows, width // 3), f32)] * 3
    return small_call(finish_qkv_kernel, "finish_qkv", outs, [info, place], pieces)


def flip_head(value):
    return lax.ppermute(value, "head", [(0, 1), (1, 0)])


def flip_dp(value, bit):
    size = lax.axis_size("dp")
    return lax.ppermute(value, "dp", [(i, i ^ (1 << bit)) for i in range(size)])


def flip_both(value, bit):
    size = lax.axis_size("dp")
    pairs = [(2 * i + h, 2 * (i ^ (1 << bit)) + 1 - h) for i in range(size) for h in range(2)]
    return lax.ppermute(value, ("dp", "head"), pairs)


def bit_of(bit):
    return (lax.axis_index("dp") >> bit) & 1


def dp_bits(first):
    return list(range(first, (lax.axis_size("dp") - 1).bit_length()))


def flip_quarter(value, number, bit):
    size = lax.axis_size("dp")
    return lax.ppermute(value, "dp", [(i, i ^ (number << bit)) for i in range(size)])


def total_of(terms):
    total = 0.0
    for term in terms:
        total = total + term.astype(f32)
    return total.astype(bf16)


def rows_of(terms, place, rows):
    return total_of([lax.dynamic_slice_in_dim(term, place * rows, rows, 0) for term in terms])


def gather_pieces(part):
    size = lax.axis_size("dp")
    one = [c + 2 * x + 4 * q for c in range(2) for x in range(2) for q in range(4)]
    groups = [[16 * k + i for i in one] for k in range(size // 16)]
    return lax.all_gather(part, "dp", axis_index_groups=groups)


def finish_quarters(kept, got):
    part, sums = settle_up([kept, *got])
    for bit in dp_bits(4):
        size = part.shape[0] // 2
        part_got = flip_dp(rows_of([part], 1 - bit_of(bit), size), bit)
        part = total_of([rows_of([part], bit_of(bit), size), part_got])
        sums = sums + flip_dp(sums, bit)
    for bit in dp_bits(4)[::-1]:
        part = join(part, flip_dp(part, bit), bit_of(bit), 0)
    return part, sums


def order(*values):
    return lax.optimization_barrier(values)


def join(mine, theirs, own, axis):
    first = jnp.where(own == 0, mine, theirs)
    second = jnp.where(own == 0, theirs, mine)
    return jnp.concatenate([first, second], axis=axis)


def body(
    hidden_in,
    w_query,
    b_query,
    w_key,
    w_value,
    b_value,
    w_out,
    b_out,
    gain_one,
    shift_one,
    w_up,
    b_up,
    w_down,
    b_down,
    gain_two,
    shift_two,
    seq_length,
    block_perm,
    cotangent,
):
    D, half = w_query.shape
    FF = w_up.shape[1]
    own = hidden_in.shape[0] // BLOCK // 2
    head = lax.axis_index("head")
    core = bit_of(0)
    mine = (w_query, w_key, w_value)

    rows = D // 2
    near = flip_head(
        jnp.concatenate([lax.dynamic_slice_in_dim(w, core * rows, rows, 0) for w in mine], 1)
    )
    w_a = jnp.concatenate(mine, 1)
    bias_a = jnp.stack([b_query, b_value])
    bias_b = flip_head(bias_a)
    perm_b = flip_head(block_perm)
    place = lax.broadcasted_iota(jnp.int32, (3,), 0)
    info = jnp.where(place == HEAD, head, jnp.where(place == CORE, core, bit_of(1))).astype(
        jnp.int32
    )
    scalars_a = (info, seq_length, block_perm)
    scalars_b = (info, seq_length, perm_b)
    zeros = jnp.zeros((D,), f32)
    consts = jnp.concatenate(
        [
            jnp.stack([b_out, gain_one, shift_one, b_down, gain_two, shift_two, zeros, zeros]),
            b_up.reshape(FF // D, D),
            jnp.zeros((8 - FF // D, D), f32),
        ]
    )

    att, q_a, kv_a = attend(scalars_a, 0, hidden_in, (w_a,), bias_a, own)
    near, att = order(near, att)
    far = flip_dp(near, 0)
    att, q_b, kv_b, w_b = attend(scalars_b, 1, hidden_in, (near, far), bias_b, own, att)

    dp = lax.axis_index("dp")
    slot = lax.broadcasted_iota(jnp.int32, (3,), 0)
    place = jnp.where(slot == 0, (dp >> 1) & 3, jnp.where(slot == 1, (dp >> 3) & 1, (dp >> 2) & 3))
    place = place.astype(jnp.int32)

    block_out, *saved, down_near, down_far, vectors = middle_up(
        info, att, hidden_in, cotangent, w_out, w_up, w_down, consts
    )
    down_far = flip_dp(down_far, 0)

    def leave(mine, sent):
        return [total_of([mine[n], sent[n]]) for n in (1, 2, 3)]

    def across(beside, over, corner):
        return [flip_both(corner, 1), flip_head(over), flip_dp(beside, 1)]

    att, *leaving = order(att, *leave(down_near, down_far))
    down = across(*leaving)
    gatt, gfirst, up_near, up_far = middle_down(
        info, att, saved, vectors, w_out, w_up, w_down, consts
    )
    gatt, up_far, *down = order(gatt, up_far, *down)
    up_far = flip_dp(up_far, 0)
    down_kept, *down = quarters(((0, FF // 4),), 2, place, [*down, down_near[0], down_far[0]])
    up_far, *down = order(up_far, *down)
    gatt, *both = order(gatt, *leave(up_near, up_far), *down)
    up = across(*both[:3])
    down = [flip_quarter(value, n + 1, 2) for n, value in enumerate(both[3:])]
    d_b, near_b, *far_b = attend_back(scalars_b, 1, q_b, kv_b, att, gatt, hidden_in, own)
    d_b, *more = order(d_b, *down, *up, *far_b)
    down, up = more[:3], more[3:6]
    far_b = [flip_dp(far, 0) for far in more[6:]]
    down = gather_pieces(finish_quarters(down_kept, down)[0])
    sections = ((0, D // 2), (D // 2, 4 * OUT_ROWS))
    up_kept, *up = quarters(sections, 2, place, [*up, up_near[0], up_far[0]])
    gatt, near_b, *up = order(gatt, join_cores(near_b, *far_b), *up)
    from_other = flip_head(near_b)
    up = [flip_quarter(value, n + 1, 2) for n, value in enumerate(up)]
    d_a, near_a, *far_a = attend_back(scalars_a, 0, q_a, kv_a, att, gatt, hidden_in, own)

    from_other, d_a, *more = order(from_other, d_a, *up, *far_a)
    up, far_a = more[:3], [flip_dp(far, 0) for far in more[3:]]
    up, vectors = finish_quarters(up_kept, up)
    up = gather_pieces(up)

    kept, *out = quarters(((0, rows),), 0, place, [near_a, from_other, *far_a])
    d_a, *out = order(d_a, *out)
    got = [flip_quarter(value, n + 1, 1) for n, value in enumerate(out)]
    input_grad, next_block = input_call(info, d_a, d_b, w_a, w_b, gfirst, own)
    input_grad, *got = order(input_grad, *got)
    kept, sent = halves(place, [kept, *got])
    next_block, sent = order(next_block, sent)
    recv = flip_head(next_block)
    part, sum_q, sum_v = settle(kept, flip_dp(sent, 3))
    for bit in dp_bits(4):
        size = part.shape[0] // 2
        part_got = flip_dp(rows_of([part], 1 - bit_of(bit), size), bit)
        part = total_of([rows_of([part], bit_of(bit), size), part_got])
        sum_q, sum_v = sum_q + flip_dp(sum_q, bit), sum_v + flip_dp(sum_v, bit)
    for bit in dp_bits(3)[::-1]:
        part = join(part, flip_dp(part, bit), bit_of(bit), 0)
    part, down = order(part, down)
    got = [flip_quarter(part, n, 1) for n in (1, 2, 3)]
    pieces = [part, *got]
    grad_down = down.reshape(FF, half).astype(f32)
    input_grad = edge_call(info, recv, input_grad, own)
    grad_down, input_grad, *pieces = order(grad_down, input_grad, *pieces)
    pieces += [flip_dp(piece, 0) for piece in pieces]
    grad_up, grad_out, sum_up, *sums = finish_up(info, vectors, up)
    grad_q, grad_k, grad_v = finish_qkv(info, place, pieces)
    return (
        block_out,
        input_grad,
        grad_q,
        sum_q,
        grad_k,
        grad_v,
        sum_v,
        grad_out,
        sums[0],
        sums[1],
        sums[2],
        grad_up,
        sum_up,
        grad_down,
        sums[3],
        sums[4],
        sums[5],
    )


def solution(mesh):
    rows = P(("dp", "head"), None)
    cols = P(None, "head")
    piece = P("head")
    return jax.shard_map(
        body,
        mesh=mesh,
        in_specs=(
            P("dp", None),
            cols,
            piece,
            cols,
            cols,
            piece,
            *[P()] * 10,
            P("dp"),
            P("dp", "head"),
            rows,
        ),
        out_specs=(
            rows,
            rows,
            cols,
            piece,
            cols,
            cols,
            piece,
            cols,
            piece,
            piece,
            piece,
            cols,
            piece,
            cols,
            piece,
            piece,
            piece,
        ),
        check_vma=False,
    )
```

```python
import functools
import math

import jax
import jax.numpy as jnp
from jax import lax
from jax.experimental import pallas as pl
from jax.experimental.pallas import tpu as pltpu
from jax.sharding import PartitionSpec as P

HEAD_DIM = 64
BLOCK = 512
PAIR = 2 * HEAD_DIM
EPS = 1e-5
SCALE = 1.0 / math.sqrt(HEAD_DIM)
bf16, f32 = jnp.bfloat16, jnp.float32
NT = (((1,), (1,)), ((), ()))
TN = (((0,), (0,)), ((), ()))
QUICK = pl.CostEstimate(flops=1000, bytes_accessed=1000, transcendentals=0)


def dot(left, right, dims=None):
    if dims is None:
        return jnp.dot(left, right, preferred_element_type=f32)
    return lax.dot_general(left, right, dims, preferred_element_type=f32)


def params(mib=40):
    return pltpu.CompilerParams(vmem_limit_bytes=mib * 1024 * 1024)


def whole(shape):
    return pl.BlockSpec(shape, lambda *_: (0,) * len(shape), pipeline_mode=pl.Buffered(1))


def colsum(values):
    return jnp.sum(values, axis=0, keepdims=True)


HEAD, CORE, NEXT = range(3)


def block_row(s, info, own):
    return jnp.where(s < own, info[HEAD] * own + s, jnp.where(info[HEAD] == 0, own, own - 1))


def key_place(own, info, length, perm, i, h):
    n = length[0] // BLOCK
    p = info[HEAD] * own + i
    c = p // n * n + perm[p, h] % n - info[HEAD] * own
    return jnp.where((c >= 0) & (c < own), c, own)


def attend_steps(own, info, length, perm, x_ref, w_ref, b_ref, att_ref, qaug_ref, kv_ref, q_scr):
    step = pl.program_id(0)
    half = q_scr.shape[2]
    heads = half // HEAD_DIM

    @pl.when(step <= own)
    def _():
        x = x_ref[...]
        kv = dot(x, w_ref[:, half:])
        kv_ref[step, :, :half] = kv[:, :half].astype(bf16)
        kv_ref[step, :, half:] = (kv[:, half:] + b_ref[1:2, :]).astype(bf16)

        @pl.when(step < own)
        def _():
            q = (dot(x, w_ref[:, :half]) + b_ref[0:1, :]).astype(bf16)
            q_scr[step] = (q.astype(f32) * SCALE).astype(bf16)

    @pl.when(step > own)
    def _():
        i = step - own - 1
        lane = lax.broadcasted_iota(jnp.int32, (BLOCK, PAIR), 1)
        low = lane < HEAD_DIM
        for pair in range(heads // 2):
            cols = slice(pair * PAIR, pair * PAIR + PAIR)
            vcols = slice(half + pair * PAIR, half + pair * PAIR + PAIR)
            q = q_scr[i, :, cols]
            outs = []
            for a in range(2):
                c = key_place(own, info, length, perm, i, 2 * pair + a)
                mine = low if a == 0 else jnp.logical_not(low)
                base = HEAD_DIM if a == 0 else 0
                k = kv_ref[c, :, cols]
                v = kv_ref[c, :, vcols]
                s = dot(jnp.where(mine, q, jnp.zeros_like(q)), k, NT)
                m = jnp.max(s, axis=1, keepdims=True)
                p = jnp.exp(s - m).astype(bf16)
                o = dot(p, jnp.where(mine, v, jnp.ones_like(v)))
                total = m + jnp.log(o)
                hi = total.astype(bf16).astype(f32)
                rest = total - hi
                mid = rest.astype(bf16).astype(f32)
                aug = jnp.where(
                    lane == base,
                    hi,
                    jnp.where(lane == base + 1, mid, jnp.where(lane == base + 2, rest - mid, 0.0)),
                )
                qaug_ref[i, 2 * pair + a] = jnp.where(mine, q, aug.astype(bf16))
                outs.append(o * pl.reciprocal(pltpu.roll(o, HEAD_DIM, 1), approx=True))
            att_ref[:, cols] = jnp.where(low, outs[0], outs[1]).astype(bf16)


def attend_own_kernel(own, info, length, perm, x, w, b, att, qaug, kv, q_scr):
    attend_steps(own, info, length, perm, x, w, b, att, qaug, kv, q_scr)


def attend_other_kernel(own, info, length, perm, x, near, far, b, _, att, qaug, kv, w, q_scr):
    rows = near.shape[0]

    @pl.when(pl.program_id(0) == 0)
    def _():
        core = info[CORE]
        w[pl.ds(pl.multiple_of(core * rows, rows), rows), :] = near[...]
        w[pl.ds(pl.multiple_of((1 - core) * rows, rows), rows), :] = far[...]

    attend_steps(own, info, length, perm, x, w, b, att, qaug, kv, q_scr)


def attend(scalars, side, x, weights, biases, own, att=None):
    D = x.shape[1]
    half = D // 2
    heads = half // HEAD_DIM
    in_specs = [
        pl.BlockSpec((BLOCK, D), lambda s, n, *_: (block_row(jnp.minimum(s, own), n, own), 0)),
        *[whole(w.shape) for w in weights],
        whole(biases.shape),
    ]
    column = lambda n: n[HEAD] if side == 0 else 1 - n[HEAD]
    out_specs = [
        pl.BlockSpec((BLOCK, half), lambda s, n, *_: (jnp.maximum(s - own - 1, 0), column(n))),
        whole((own, heads, BLOCK, PAIR)),
        whole((own + 1, BLOCK, 2 * half)),
    ]
    out_shape = [
        jax.ShapeDtypeStruct((own * BLOCK, D), bf16),
        jax.ShapeDtypeStruct((own, heads, BLOCK, PAIR), bf16),
        jax.ShapeDtypeStruct((own + 1, BLOCK, 2 * half), bf16),
    ]
    operands = [*scalars, x, *weights, biases]
    aliases = {}
    if att is None:
        body = attend_own_kernel
    else:
        body = attend_other_kernel
        in_specs.append(pl.BlockSpec(memory_space=pl.ANY))
        operands.append(att)
        aliases = {len(operands) - 1: 0}
        out_specs.append(whole((D, 3 * half)))
        out_shape.append(jax.ShapeDtypeStruct((D, 3 * half), bf16))
    return pl.pallas_call(
        functools.partial(body, own),
        grid_spec=pltpu.PrefetchScalarGridSpec(
            num_scalar_prefetch=3,
            grid=(2 * own + 1,),
            in_specs=in_specs,
            out_specs=out_specs,
            scratch_shapes=[pltpu.VMEM((own, BLOCK, half), bf16)],
        ),
        out_shape=out_shape,
        input_output_aliases=aliases,
        compiler_params=params(),
        cost_estimate=QUICK,
        name="attend_forward",
    )(*operands)


def attend_back_kernel(
    own,
    info,
    length,
    perm,
    qaug_ref,
    kv_ref,
    att_ref,
    do_ref,
    x_ref,
    d_ref,
    near_ref,
    left_ref,
    right_ref,
    x_scr,
):
    step = pl.program_id(0)
    heads = qaug_ref.shape[1]
    half = heads * HEAD_DIM

    @pl.when(step == 0)
    def _():
        d_ref[...] = jnp.zeros_like(d_ref)

    x_scr[pl.ds(pl.multiple_of(step * BLOCK, BLOCK), BLOCK), :] = x_ref[...]

    @pl.when(step < own)
    def _():
        lane = lax.broadcasted_iota(jnp.int32, (BLOCK, PAIR), 1)
        low = lane < HEAD_DIM
        here = pl.ds(pl.multiple_of(step * BLOCK, BLOCK), BLOCK)
        for pair in range(heads // 2):
            cols = slice(pair * PAIR, pair * PAIR + PAIR)
            kcols = slice(half + pair * PAIR, half + pair * PAIR + PAIR)
            vcols = slice(2 * half + pair * PAIR, 2 * half + pair * PAIR + PAIR)
            do = do_ref[:, cols]
            prod = do.astype(f32) * att_ref[:, cols].astype(f32)
            dqs = []
            for a in range(2):
                c = key_place(own, info, length, perm, step, 2 * pair + a)
                mine = low if a == 0 else jnp.logical_not(low)
                base = HEAD_DIM if a == 0 else 0
                delta = jnp.sum(jnp.where(mine, prod, 0.0), axis=1, keepdims=True)
                hi = delta.astype(bf16).astype(f32)
                aug = jnp.where(lane == base, hi, jnp.where(lane == base + 1, delta - hi, 0.0))
                doaug = jnp.where(mine, do, aug.astype(bf16))
                k = kv_ref[c, :, cols]
                v = kv_ref[c, :, kcols]
                extra = jnp.where((lane >= base) & (lane < base + 3), -1.0, 0.0).astype(bf16)
                q = qaug_ref[0, 2 * pair + a]
                p = jnp.exp(dot(jnp.where(mine, k, extra), q, NT))
                ds = (p * dot(jnp.where(mine, v, extra), doaug, NT)).astype(bf16)
                dv = dot(p.astype(bf16), do).astype(bf16)
                dk = dot(ds, q).astype(bf16)
                dqs.append(dot(ds, k, TN) * SCALE)
                there = pl.ds(pl.multiple_of(c * BLOCK, BLOCK), BLOCK)
                d_ref[there, kcols] = jnp.where(mine, dk, d_ref[there, kcols])
                d_ref[there, vcols] = jnp.where(mine, dv, d_ref[there, vcols])
            d_ref[here, cols] = jnp.where(low, dqs[0], dqs[1]).astype(bf16)

    @pl.when(step == own)
    def _():
        core = info[CORE]
        d = d_ref[...]
        more = near_ref.shape[0] - half
        row = lax.broadcasted_iota(jnp.int32, (more, d.shape[1]), 0)
        sums = jnp.where(row == 0, colsum(d.astype(f32)), 0.0).astype(bf16)
        width = left_ref.shape[1]
        near_ref[half:, :] = sums
        left_ref[half:, :] = sums[:, :width]
        right_ref[half:, :] = sums[:, width:]
        x = x_scr[:, pl.ds(pl.multiple_of((1 - core) * half, half), half)]
        far = dot(x, d, TN).astype(bf16)
        left_ref[:half, :] = far[:, :width]
        right_ref[:half, :] = far[:, width:]
        x = x_scr[:, pl.ds(pl.multiple_of(core * half, half), half)]
        near_ref[:half, :] = dot(x, d, TN).astype(bf16)


def attend_back(scalars, side, qaug, kv, att, do, x, own):
    heads = qaug.shape[1]
    half = heads * HEAD_DIM
    D = x.shape[1]
    column = lambda n: n[HEAD] if side == 0 else 1 - n[HEAD]
    last = own - 1
    rows = pl.BlockSpec((BLOCK, half), lambda s, n, *_: (jnp.minimum(s, last), column(n)))
    d_shape = ((own + 1) * BLOCK, 3 * half)
    w_shape = (D // 2 + 16, 3 * half)
    w_parts = [(D // 2 + 16, width) for width in (2 * half - PAIR, half + PAIR)]
    return pl.pallas_call(
        functools.partial(attend_back_kernel, own),
        grid_spec=pltpu.PrefetchScalarGridSpec(
            num_scalar_prefetch=3,
            grid=(own + 1,),
            in_specs=[
                pl.BlockSpec(
                    (1, heads, BLOCK, PAIR), lambda s, *_: (jnp.minimum(s, last), 0, 0, 0)
                ),
                whole(kv.shape),
                rows,
                rows,
                pl.BlockSpec((BLOCK, D), lambda s, n, *_: (block_row(s, n, own), 0)),
            ],
            out_specs=[whole(d_shape), whole(w_shape), *[whole(w) for w in w_parts]],
            scratch_shapes=[pltpu.VMEM(((own + 1) * BLOCK, D), bf16)],
        ),
        out_shape=[
            jax.ShapeDtypeStruct(d_shape, bf16),
            jax.ShapeDtypeStruct(w_shape, bf16),
            *[jax.ShapeDtypeStruct(w, bf16) for w in w_parts],
        ],
        compiler_params=params(),
        cost_estimate=QUICK,
        name="attend_backward",
    )(*scalars, qaug, kv, att, do, x)


def norm_terms(z):
    mean = jnp.mean(z, axis=1, keepdims=True)
    centred = z - mean
    variance = jnp.mean(centred * centred, axis=1, keepdims=True)
    inverse = lax.rsqrt(variance + EPS)
    return centred * inverse, inverse


def norm_back(incoming, normed, inverse, gain):
    scaled = incoming * gain
    first = jnp.mean(scaled, axis=1, keepdims=True)
    second = jnp.mean(scaled * normed, axis=1, keepdims=True)
    return inverse * (scaled - first - normed * second)


def gelu_parts(v):
    cdf = 0.5 + 0.5 * lax.erf(v * math.sqrt(0.5))
    return v * cdf, cdf + v * (math.sqrt(0.5 / math.pi) * jnp.exp(v * (v * -0.5)))


def add_up(acc, rows, cols, value):
    first = pl.program_id(0) == 0
    acc[rows, cols] = jnp.where(first, value, value + acc[rows, cols])


OUT_ROWS = 32


def place_piece(info, c, y, x, near_ref, far_ref, rows, cols, piece):
    number = (info[HEAD] ^ y) * 2 + (info[NEXT] ^ x)

    @pl.when(info[CORE] == c)
    def _():
        near_ref[number, rows, cols] = piece

    @pl.when(info[CORE] != c)
    def _():
        far_ref[number, rows, cols] = piece


def middle_up_kernel(
    info,
    att_ref,
    x_ref,
    cot_ref,
    c_ref,
    wo_ref,
    wu_ref,
    wd_ref,
    out_ref,
    slope_ref,
    n1_ref,
    inv_ref,
    gsec_ref,
    near_ref,
    far_ref,
    vec_ref,
    act_scr,
    acc,
):
    i = pl.program_id(0)
    D, ff = wu_ref.shape
    bo, g1, s1, bd, g2, s2 = (c_ref[r : r + 1, :] for r in range(6))
    branch = dot(att_ref[...], wo_ref[...]) + bo
    n1, inv1 = norm_terms(x_ref[...].astype(f32) + branch)
    n1_ref[...] = n1
    inv_ref[...] = jnp.broadcast_to(inv1, inv_ref.shape)
    y1 = n1 * g1 + s1
    upin = y1.astype(bf16)
    ffn = bd
    for f in range(ff // D):
        cols = slice(f * D, f * D + D)
        value, slope = gelu_parts(dot(upin, wu_ref[:, cols]) + c_ref[8 + f : 9 + f, :])
        act = value.astype(bf16)
        act_scr[:, cols] = act
        slope_ref[:, cols] = slope.astype(bf16)
        ffn = ffn + dot(act, wd_ref[cols, :])
    n2, inv2 = norm_terms(y1 + ffn)
    out_ref[...] = (n2 * g2 + s2).astype(bf16)
    e = cot_ref[...].astype(f32)
    gsec = norm_back(e, n2, inv2, g2)
    gsec_ref[...] = gsec
    gffn = gsec.astype(bf16)
    for f in range(ff // D):
        cols = slice(f * D, f * D + D)
        add_up(acc, cols, slice(None), dot(act_scr[:, cols], gffn, TN))

    @pl.when(i == 0)
    def _():
        vec_ref[...] = jnp.zeros_like(vec_ref)

    for row, values in ((3, gffn.astype(f32)), (4, e * n2), (5, e)):
        vec_ref[row : row + 1, :] += colsum(values)

    @pl.when(i == pl.num_programs(0) - 1)
    def _():
        half = D // 2
        for f in range(ff // D):
            for y in range(2):
                piece = acc[f * D : f * D + D, y * half : y * half + half].astype(bf16)
                place_piece(
                    info, f // 2, y, f % 2, near_ref, far_ref, slice(None), slice(None), piece
                )


def middle_up(info, att, x, cot, wo, wu, wd, consts, tile=BLOCK // 2):
    R, D = att.shape
    FF = wu.shape[1]
    tiles = R // tile
    row = lambda width: pl.BlockSpec((tile, width), lambda s, n: (s, 0))
    kept = pl.BlockSpec(memory_space=pltpu.VMEM)
    sd = jax.ShapeDtypeStruct
    pieces = (4, FF // 4, D // 2)
    return pl.pallas_call(
        middle_up_kernel,
        grid_spec=pltpu.PrefetchScalarGridSpec(
            num_scalar_prefetch=1,
            grid=(tiles,),
            in_specs=[
                row(D),
                pl.BlockSpec((tile, D), lambda s, n: (s + n[HEAD] * tiles, 0)),
                row(D),
                whole(consts.shape),
                kept,
                kept,
                kept,
            ],
            out_specs=[row(D), row(FF), row(D), row(128), row(D)]
            + [whole(pieces), whole(pieces), whole(consts.shape)],
            scratch_shapes=[
                pltpu.VMEM((tile, FF), bf16),
                pltpu.VMEM((FF, D), f32),
            ],
        ),
        out_shape=[
            sd((R, D), bf16),
            sd((R, FF), bf16),
            sd((R, D), f32),
            sd((R, 128), f32),
            sd((R, D), f32),
            sd(pieces, bf16),
            sd(pieces, bf16),
            sd(consts.shape, f32),
        ],
        compiler_params=params(44),
        cost_estimate=QUICK,
        name="middle_up",
    )(info, att, x, cot, consts, wo, wu, wd)


def middle_down_kernel(
    info,
    att_ref,
    slope_ref,
    n1_ref,
    inv_ref,
    gsec_ref,
    vec_in_ref,
    c_ref,
    wo_ref,
    wu_ref,
    wd_ref,
    gatt_ref,
    gfirst_ref,
    near_ref,
    far_ref,
    vec_ref,
    gp_scr,
    acc,
    acc_out,
):
    i = pl.program_id(0)
    D, ff = wu_ref.shape

    @pl.when(i == 0)
    def _():
        vec_ref[...] = vec_in_ref[...]

    g1, s1 = c_ref[1:2, :], c_ref[2:3, :]
    n1 = n1_ref[...]
    upin = (n1 * g1 + s1).astype(bf16)
    gsec = gsec_ref[...]
    gffn = gsec.astype(bf16)
    for f in range(ff // D):
        cols = slice(f * D, f * D + D)
        gp = (dot(gffn, wd_ref[cols, :], NT) * slope_ref[:, cols].astype(f32)).astype(bf16)
        gp_scr[:, cols] = gp
        vec_ref[8 + f : 9 + f, :] += colsum(gp.astype(f32))
    gnormed = gsec
    for f in range(ff // D):
        cols = slice(f * D, f * D + D)
        gp = gp_scr[:, cols]
        gnormed = gnormed + dot(gp, wu_ref[:, cols], NT)
        add_up(acc, slice(None), cols, dot(upin, gp, TN))
    gfirst = norm_back(gnormed, n1, inv_ref[:, :1], g1)
    gfirst_ref[...] = gfirst
    gbr = gfirst.astype(bf16)
    gatt_ref[...] = dot(gbr, wo_ref[...], NT).astype(bf16)
    add_up(acc_out, slice(None), slice(None), dot(gbr, att_ref[...], TN))
    for row, values in enumerate((gbr.astype(f32), gnormed * n1, gnormed)):
        vec_ref[row : row + 1, :] += colsum(values)

    @pl.when(i == pl.num_programs(0) - 1)
    def _():
        half, few = D // 2, D // 32
        for f in range(ff // D):
            for x in range(2):
                piece = acc[x * half : x * half + half, f * D : f * D + D].astype(bf16)
                place_piece(
                    info, f % 2, f // 2, x, near_ref, far_ref, slice(0, half), slice(None), piece
                )
        sums = vec_ref[...].astype(bf16)
        for number in range(4):
            near_ref[number, half + 4 * OUT_ROWS :, :] = sums
            far_ref[number, half + 4 * OUT_ROWS :, :] = sums
        for c in range(2):
            for y in range(2):
                for x in range(2):
                    for q in range(4):
                        top = (8 * y + 4 * x + q) * 2 * few
                        both = acc_out[top : top + 2 * few, c * half : c * half + half]
                        both = jnp.concatenate([both[:few], both[few:]], axis=1)
                        pad = jnp.zeros((OUT_ROWS - few, D), f32)
                        both = jnp.concatenate([both, pad], axis=0).astype(bf16)
                        rows = slice(half + q * OUT_ROWS, half + q * OUT_ROWS + OUT_ROWS)
                        place_piece(info, c, y, x, near_ref, far_ref, rows, slice(None), both)


def middle_down(info, att, saved, vectors, wo, wu, wd, consts, tile=BLOCK // 2):
    R, D = att.shape
    FF = wu.shape[1]
    row = lambda width: pl.BlockSpec((tile, width), lambda s, n: (s, 0))
    kept = pl.BlockSpec(memory_space=pltpu.VMEM)
    sd = jax.ShapeDtypeStruct
    pieces = (4, D // 2 + 4 * OUT_ROWS + consts.shape[0], FF // 4)
    return pl.pallas_call(
        middle_down_kernel,
        grid_spec=pltpu.PrefetchScalarGridSpec(
            num_scalar_prefetch=1,
            grid=(R // tile,),
            in_specs=[row(D), row(FF), row(D), row(128), row(D)]
            + [whole(consts.shape)] * 2
            + [kept] * 3,
            out_specs=[row(D), row(D), whole(pieces), whole(pieces)],
            scratch_shapes=[
                pltpu.VMEM(consts.shape, f32),
                pltpu.VMEM((tile, FF), bf16),
                pltpu.VMEM((D, FF), f32),
                pltpu.VMEM((D, D), f32),
            ],
        ),
        out_shape=[
            sd((R, D), bf16),
            sd((R, D), f32),
            sd(pieces, bf16),
            sd(pieces, bf16),
        ],
        compiler_params=params(44),
        cost_estimate=QUICK,
        name="middle_down",
    )(info, att, *saved, vectors, consts, wo, wu, wd)


def input_kernel(own, info, da, db, wa, wb, first, out_ref, next_ref):
    total = dot(da[...], wa[...], NT) + dot(db[...], wb[...], NT)

    @pl.when(pl.program_id(0) == 0)
    def _():
        next_ref[...] = total.astype(bf16)

    @pl.when(pl.program_id(0) > 0)
    def _():
        out_ref[...] = total + first[...]


def input_call(info, da, db, wa, wb, first, own):
    D, width = wa.shape
    row = pl.BlockSpec((BLOCK, width), lambda s, n: (jnp.where(s == 0, own, s - 1), 0))
    wide = pl.BlockSpec((BLOCK, D), lambda s, n: (jnp.maximum(s - 1, 0), 0))
    return pl.pallas_call(
        functools.partial(input_kernel, own),
        grid_spec=pltpu.PrefetchScalarGridSpec(
            num_scalar_prefetch=1,
            grid=(own + 1,),
            in_specs=[row, row, whole((D, width)), whole((D, width)), wide],
            out_specs=[wide, whole((BLOCK, D))],
        ),
        out_shape=[
            jax.ShapeDtypeStruct(first.shape, f32),
            jax.ShapeDtypeStruct((BLOCK, D), bf16),
        ],
        compiler_params=params(60),
        cost_estimate=QUICK,
        name="input_grad",
    )(info, da, db, wa, wb, first)


def edge_kernel(info, recv, rest, out_ref):
    out_ref[...] = rest[...] + recv[...].astype(f32)


def edge_call(info, recv, rest, own):
    D = rest.shape[1]
    edge = pl.BlockSpec((BLOCK // 4, D), lambda s, n: (s + 4 * jnp.where(n[HEAD] == 0, own - 1, 0), 0))
    return pl.pallas_call(
        edge_kernel,
        grid_spec=pltpu.PrefetchScalarGridSpec(
            num_scalar_prefetch=1,
            grid=(4,),
            in_specs=[pl.BlockSpec((BLOCK // 4, D), lambda s, n: (s, 0)), edge],
            out_specs=edge,
        ),
        out_shape=jax.ShapeDtypeStruct(rest.shape, f32),
        input_output_aliases={2: 0},
        compiler_params=params(),
        cost_estimate=QUICK,
        name="edge_block",
    )(info, recv, rest)


def finish_up_kernel(info, vec_in_ref, parts, *refs):
    up_ref, out_ref, sums_ref, *vec_refs, scr = refs
    width = parts.shape[2]
    half, few = width // 2, width // 32
    count = parts.shape[0] // 4
    rows, size = half // count, parts.shape[1]
    for c in range(2):
        for x in range(2):
            for q in range(count):
                piece = parts[(2 * c + x) * count + q].astype(f32)
                up_ref[
                    x * half + q * rows : x * half + q * rows + rows, c * width : c * width + width
                ] = piece[:rows]
                for n in range(2):
                    top = x * (half // 2) + (2 * q + n) * few
                    scr[top : top + few, c * half : c * half + half] = piece[
                        rows : rows + few, n * half : n * half + half
                    ]
    out_ref[...] = scr[...].T
    vectors = vec_in_ref[...].astype(f32)
    mine = jnp.where(info[HEAD] == 0, vectors[:, :half], vectors[:, half:])
    for row, ref in enumerate(vec_refs):
        ref[...] = mine[row]
    chunks = sums_ref.shape[0] // width
    for n in range(chunks):
        both = jnp.where(info[HEAD] == 0, vectors[8 + n], vectors[8 + chunks + n])
        sums_ref[n * width : n * width + width] = both


def finish_up(info, vectors, parts):
    width = parts.shape[2]
    outs = [
        ((width, 2 * width), f32),
        ((width, width // 2), f32),
        ((2 * width,), f32),
        *[((width // 2,), f32)] * 6,
    ]
    scratch = [pltpu.VMEM((width // 2, width), f32)]
    return small_call(finish_up_kernel, "finish_up", outs, [info], [vectors, parts], scratch, True)


def small_call(kernel, name, outs, scalars, arrays, scratch=(), whole_arrays=False, mib=40):
    smem = pl.BlockSpec(memory_space=pltpu.SMEM)

    def spec(array):
        if array.ndim < 3 or whole_arrays:
            return whole(array.shape)
        shape = (None, *array.shape[1:])
        return pl.BlockSpec(shape, lambda _: (0, 0, 0), pipeline_mode=pl.Buffered(1))

    return pl.pallas_call(
        kernel,
        grid=(1,),
        in_specs=[smem] * len(scalars) + [spec(array) for array in arrays],
        out_specs=[whole(shape) for shape, _ in outs],
        out_shape=[jax.ShapeDtypeStruct(shape, kind) for shape, kind in outs],
        scratch_shapes=list(scratch),
        compiler_params=params(mib),
        cost_estimate=QUICK,
        name=name,
    )(*scalars, *arrays)


def quarters_kernel(sections, at, place, *refs):
    terms, outs = refs[:-4], refs[-4:]
    for n, out in enumerate(outs):
        done = 0
        parts = [(start + (place[at] ^ n) * (rows // 4), rows // 4) for start, rows in sections]
        for top, rows in parts + [(sum(sections[-1]), 16)]:
            if not isinstance(top, int):
                top = pl.multiple_of(top, 16)
            values = [term[pl.ds(top, rows), :].astype(f32) for term in terms]
            if values[-1].shape[1] < out.shape[1]:
                values[-2:] = [jnp.concatenate(values[-2:], axis=1)]
            out[done : done + rows, :] = sum(values).astype(out.dtype)
            done += rows


def quarters(sections, at, place, terms):
    rows, width = sum(rows // 4 for _, rows in sections) + 16, terms[0].shape[1]
    outs = [((rows, width), f32)] + [((rows, width), bf16)] * 3
    kernel = functools.partial(quarters_kernel, sections, at)
    return small_call(kernel, "quarters", outs, [place], terms, mib=60)


def join_cores_kernel(near, left, right, out):
    far = jnp.concatenate([left[...].astype(f32), right[...].astype(f32)], axis=1)
    out[...] = (near[...].astype(f32) + far).astype(bf16)


def join_cores(near, left, right):
    outs = [(near.shape, bf16)]
    return small_call(join_cores_kernel, "join_cores", outs, [], [near, left, right])[0]


def settle_up_kernel(*refs):
    terms, (part, vectors) = refs[:-2], refs[-2:]
    rows = part.shape[0]
    part[...] = sum(term[:rows, :].astype(f32) for term in terms).astype(bf16)
    vectors[...] = sum(term[rows:, :].astype(f32) for term in terms)


def settle_up(terms):
    rows, width = terms[0].shape
    outs = [((rows - 16, width), bf16), ((16, width), f32)]
    return small_call(settle_up_kernel, "settle_up", outs, [], terms)


def halves_kernel(place, *refs):
    terms, (kept, sent, scr) = refs[:4], refs[4:]
    few = kept.shape[0] - 16
    scr[...] = sum(term[...].astype(f32) for term in terms)
    for out, which in ((kept, place[1]), (sent, 1 - place[1])):
        out[:few, :] = scr[pl.ds(pl.multiple_of(which * few, 16), few), :].astype(out.dtype)
        out[few:, :] = scr[2 * few :, :].astype(out.dtype)


def halves(place, terms):
    rows, width = terms[0].shape
    shape = ((rows - 16) // 2 + 16, width)
    scratch = [pltpu.VMEM((rows, width), f32)]
    return small_call(
        halves_kernel, "halves", [(shape, f32), (shape, bf16)], [place], terms, scratch
    )


def settle_kernel(kept, got, part, q_sum, v_sum):
    few, width = part.shape
    half = width // 3
    total = kept[...] + got[...].astype(f32)
    part[...] = total[:few].astype(bf16)
    q_sum[...] = total[few, :half]
    v_sum[...] = total[few, 2 * half :]


def settle(kept, got):
    rows, width = kept.shape
    outs = [((rows - 16, width), bf16), ((width // 3,), f32), ((width // 3,), f32)]
    return small_call(settle_kernel, "settle", outs, [], [kept, got])


def finish_qkv_kernel(info, place, *refs):
    pieces, outs = refs[:8], refs[8:]
    rows = pieces[0].shape[0]
    half = outs[0].shape[1]
    for n, ref in enumerate(pieces):
        core = info[CORE] ^ (n // 4)
        top = pl.multiple_of((4 * core + (place[0] ^ (n % 4))) * rows, 8)
        piece = ref[...].astype(f32)
        for m, out in enumerate(outs):
            out[pl.ds(top, rows), :] = piece[:, m * half : m * half + half]


def finish_qkv(info, place, pieces):
    rows, width = pieces[0].shape
    outs = [((8 * rows, width // 3), f32)] * 3
    return small_call(finish_qkv_kernel, "finish_qkv", outs, [info, place], pieces)


def flip_head(value):
    return lax.ppermute(value, "head", [(0, 1), (1, 0)])


def flip_dp(value, bit):
    size = lax.axis_size("dp")
    return lax.ppermute(value, "dp", [(i, i ^ (1 << bit)) for i in range(size)])


def flip_both(value, bit):
    size = lax.axis_size("dp")
    pairs = [(2 * i + h, 2 * (i ^ (1 << bit)) + 1 - h) for i in range(size) for h in range(2)]
    return lax.ppermute(value, ("dp", "head"), pairs)


def bit_of(bit):
    return (lax.axis_index("dp") >> bit) & 1


def dp_bits(first):
    return list(range(first, (lax.axis_size("dp") - 1).bit_length()))


def flip_quarter(value, number, bit):
    size = lax.axis_size("dp")
    return lax.ppermute(value, "dp", [(i, i ^ (number << bit)) for i in range(size)])


def total_of(terms):
    total = 0.0
    for term in terms:
        total = total + term.astype(f32)
    return total.astype(bf16)


def rows_of(terms, place, rows):
    return total_of([lax.dynamic_slice_in_dim(term, place * rows, rows, 0) for term in terms])


def gather_pieces(part):
    size = lax.axis_size("dp")
    one = [c + 2 * x + 4 * q for c in range(2) for x in range(2) for q in range(4)]
    groups = [[16 * k + i for i in one] for k in range(size // 16)]
    return lax.all_gather(part, "dp", axis_index_groups=groups)


def scatter_rest(part):
    size = lax.axis_size("dp")
    groups = [[i + 4 * k for k in range(size // 4)] for i in range(4)]
    return lax.psum_scatter(part, "dp", axis_index_groups=groups, tiled=True)


def gather_all(part):
    size = lax.axis_size("dp")
    group = [c + 2 * x + 4 * k for c in range(2) for x in range(2) for k in range(size // 4)]
    return lax.all_gather(part, "dp", axis_index_groups=[group])


def finish_quarters(kept, got):
    part, sums = settle_up([kept, *got])
    for bit in dp_bits(4):
        size = part.shape[0] // 2
        part_got = flip_dp(rows_of([part], 1 - bit_of(bit), size), bit)
        part = total_of([rows_of([part], bit_of(bit), size), part_got])
        sums = sums + flip_dp(sums, bit)
    for bit in dp_bits(4)[::-1]:
        part = join(part, flip_dp(part, bit), bit_of(bit), 0)
    return part, sums


def order(*values):
    return lax.optimization_barrier(values)


def join(mine, theirs, own, axis):
    first = jnp.where(own == 0, mine, theirs)
    second = jnp.where(own == 0, theirs, mine)
    return jnp.concatenate([first, second], axis=axis)


def body(
    hidden_in,
    w_query,
    b_query,
    w_key,
    w_value,
    b_value,
    w_out,
    b_out,
    gain_one,
    shift_one,
    w_up,
    b_up,
    w_down,
    b_down,
    gain_two,
    shift_two,
    seq_length,
    block_perm,
    cotangent,
):
    D, half = w_query.shape
    FF = w_up.shape[1]
    own = hidden_in.shape[0] // BLOCK // 2
    head = lax.axis_index("head")
    core = bit_of(0)
    mine = (w_query, w_key, w_value)

    rows = D // 2
    near = flip_head(
        jnp.concatenate([lax.dynamic_slice_in_dim(w, core * rows, rows, 0) for w in mine], 1)
    )
    w_a = jnp.concatenate(mine, 1)
    bias_a = jnp.stack([b_query, b_value])
    bias_b = flip_head(bias_a)
    perm_b = flip_head(block_perm)
    place = lax.broadcasted_iota(jnp.int32, (3,), 0)
    info = jnp.where(place == HEAD, head, jnp.where(place == CORE, core, bit_of(1))).astype(
        jnp.int32
    )
    scalars_a = (info, seq_length, block_perm)
    scalars_b = (info, seq_length, perm_b)
    zeros = jnp.zeros((D,), f32)
    consts = jnp.concatenate(
        [
            jnp.stack([b_out, gain_one, shift_one, b_down, gain_two, shift_two, zeros, zeros]),
            b_up.reshape(FF // D, D),
            jnp.zeros((8 - FF // D, D), f32),
        ]
    )

    att, q_a, kv_a = attend(scalars_a, 0, hidden_in, (w_a,), bias_a, own)
    near, att = order(near, att)
    far = flip_dp(near, 0)
    att, q_b, kv_b, w_b = attend(scalars_b, 1, hidden_in, (near, far), bias_b, own, att)

    dp = lax.axis_index("dp")
    slot = lax.broadcasted_iota(jnp.int32, (3,), 0)
    place = jnp.where(slot == 0, (dp >> 1) & 3, jnp.where(slot == 1, (dp >> 3) & 1, (dp >> 2) & 3))
    place = place.astype(jnp.int32)

    block_out, *saved, down_near, down_far, vectors = middle_up(
        info, att, hidden_in, cotangent, w_out, w_up, w_down, consts
    )
    down_far = flip_dp(down_far, 0)

    def leave(mine, sent):
        return [total_of([mine[n], sent[n]]) for n in (1, 2, 3)]

    def across(beside, over, corner):
        return [flip_both(corner, 1), flip_head(over), flip_dp(beside, 1)]

    att, *leaving = order(att, *leave(down_near, down_far))
    down = across(*leaving)
    gatt, gfirst, up_near, up_far = middle_down(
        info, att, saved, vectors, w_out, w_up, w_down, consts
    )
    gatt, up_far, *down = order(gatt, up_far, *down)
    up_far = flip_dp(up_far, 0)
    down = total_of([*down, down_near[0], down_far[0]])
    up_far, down = order(up_far, down)
    down = scatter_rest(down)
    gatt, *up = order(gatt, *leave(up_near, up_far))
    up = across(*up)
    d_b, near_b, *far_b = attend_back(scalars_b, 1, q_b, kv_b, att, gatt, hidden_in, own)
    d_b, down, *more = order(d_b, down, *up, *far_b)
    up, far_b = more[:3], [flip_dp(far, 0) for far in more[3:]]
    sections = ((0, D // 2), (D // 2, 4 * OUT_ROWS))
    up_kept, *up = quarters(sections, 2, place, [*up, up_near, up_far])
    gatt, near_b, *up = order(gatt, join_cores(near_b, *far_b), *up)
    from_other = flip_head(near_b)
    up = [flip_quarter(value, n + 1, 2) for n, value in enumerate(up)]
    down = gather_all(down)
    d_a, near_a, *far_a = attend_back(scalars_a, 0, q_a, kv_a, att, gatt, hidden_in, own)

    from_other, d_a, *more = order(from_other, d_a, *up, *far_a)
    up, far_a = more[:3], [flip_dp(far, 0) for far in more[3:]]
    up, vectors = finish_quarters(up_kept, up)
    up = gather_pieces(up)

    kept, *out = quarters(((0, rows),), 0, place, [near_a, from_other, *far_a])
    d_a, *out = order(d_a, *out)
    got = [flip_quarter(value, n + 1, 1) for n, value in enumerate(out)]
    input_grad, next_block = input_call(info, d_a, d_b, w_a, w_b, gfirst, own)
    input_grad, *got = order(input_grad, *got)
    kept, sent = halves(place, [kept, *got])
    next_block, sent = order(next_block, sent)
    recv = flip_head(next_block)
    part, sum_q, sum_v = settle(kept, flip_dp(sent, 3))
    for bit in dp_bits(4):
        size = part.shape[0] // 2
        part_got = flip_dp(rows_of([part], 1 - bit_of(bit), size), bit)
        part = total_of([rows_of([part], bit_of(bit), size), part_got])
        sum_q, sum_v = sum_q + flip_dp(sum_q, bit), sum_v + flip_dp(sum_v, bit)
    for bit in dp_bits(3)[::-1]:
        part = join(part, flip_dp(part, bit), bit_of(bit), 0)
    part, down = order(part, down)
    got = [flip_quarter(part, n, 1) for n in (1, 2, 3)]
    grad_down = down.reshape(FF, half).astype(f32)
    grad_down, recv, *got = order(grad_down, recv, *got)
    pieces = [part, *got]
    got = [flip_dp(piece, 0) for piece in pieces]
    input_grad = edge_call(info, recv, input_grad, own)
    input_grad, *got = order(input_grad, *got)
    pieces += got
    grad_q, grad_k, grad_v = finish_qkv(info, place, pieces)
    grad_q, up, vectors = order(grad_q, up, vectors)
    grad_up, grad_out, sum_up, *sums = finish_up(info, vectors, up)
    return (
        block_out,
        input_grad,
        grad_q,
        sum_q,
        grad_k,
        grad_v,
        sum_v,
        grad_out,
        sums[0],
        sums[1],
        sums[2],
        grad_up,
        sum_up,
        grad_down,
        sums[3],
        sums[4],
        sums[5],
    )


def solution(mesh):
    rows = P(("dp", "head"), None)
    cols = P(None, "head")
    piece = P("head")
    return jax.shard_map(
        body,
        mesh=mesh,
        in_specs=(
            P("dp", None),
            cols,
            piece,
            cols,
            cols,
            piece,
            *[P()] * 10,
            P("dp"),
            P("dp", "head"),
            rows,
        ),
        out_specs=(
            rows,
            rows,
            cols,
            piece,
            cols,
            cols,
            piece,
            cols,
            piece,
            piece,
            piece,
            cols,
            piece,
            cols,
            piece,
            piece,
            piece,
        ),
        check_vma=False,
    )
```

```python
import functools
import math

import jax
import jax.numpy as jnp
from jax import lax
from jax.experimental import pallas as pl
from jax.experimental.pallas import tpu as pltpu
from jax.sharding import PartitionSpec as P

HEAD_DIM = 64
BLOCK = 512
PAIR = 2 * HEAD_DIM
EPS = 1e-5
SCALE = 1.0 / math.sqrt(HEAD_DIM)
bf16, f32 = jnp.bfloat16, jnp.float32
NT = (((1,), (1,)), ((), ()))
TN = (((0,), (0,)), ((), ()))
QUICK = pl.CostEstimate(flops=1000, bytes_accessed=1000, transcendentals=0)


def dot(left, right, dims=None):
    if dims is None:
        return jnp.dot(left, right, preferred_element_type=f32)
    return lax.dot_general(left, right, dims, preferred_element_type=f32)


def params(mib=40):
    return pltpu.CompilerParams(vmem_limit_bytes=mib * 1024 * 1024)


def whole(shape):
    return pl.BlockSpec(shape, lambda *_: (0,) * len(shape), pipeline_mode=pl.Buffered(1))


def colsum(values):
    return jnp.sum(values, axis=0, keepdims=True)


HEAD, CORE, NEXT = range(3)


def block_row(s, info, own):
    return jnp.where(s < own, info[HEAD] * own + s, jnp.where(info[HEAD] == 0, own, own - 1))


def key_place(own, info, length, perm, i, h):
    n = length[0] // BLOCK
    p = info[HEAD] * own + i
    c = p // n * n + perm[p, h] % n - info[HEAD] * own
    return jnp.where((c >= 0) & (c < own), c, own)


def attend_steps(own, info, length, perm, x_ref, w_ref, b_ref, att_ref, qaug_ref, kv_ref, q_scr):
    step = pl.program_id(0)
    half = q_scr.shape[2]
    heads = half // HEAD_DIM

    @pl.when(step <= own)
    def _():
        x = x_ref[...]
        kv = dot(x, w_ref[:, half:])
        kv_ref[step, :, :half] = kv[:, :half].astype(bf16)
        kv_ref[step, :, half:] = (kv[:, half:] + b_ref[1:2, :]).astype(bf16)

        @pl.when(step < own)
        def _():
            q = (dot(x, w_ref[:, :half]) + b_ref[0:1, :]).astype(bf16)
            q_scr[step] = (q.astype(f32) * SCALE).astype(bf16)

    @pl.when(step > own)
    def _():
        i = step - own - 1
        lane = lax.broadcasted_iota(jnp.int32, (BLOCK, PAIR), 1)
        low = lane < HEAD_DIM
        for pair in range(heads // 2):
            cols = slice(pair * PAIR, pair * PAIR + PAIR)
            vcols = slice(half + pair * PAIR, half + pair * PAIR + PAIR)
            q = q_scr[i, :, cols]
            outs = []
            for a in range(2):
                c = key_place(own, info, length, perm, i, 2 * pair + a)
                mine = low if a == 0 else jnp.logical_not(low)
                base = HEAD_DIM if a == 0 else 0
                k = kv_ref[c, :, cols]
                v = kv_ref[c, :, vcols]
                s = dot(jnp.where(mine, q, jnp.zeros_like(q)), k, NT)
                m = jnp.max(s, axis=1, keepdims=True)
                p = jnp.exp(s - m).astype(bf16)
                o = dot(p, jnp.where(mine, v, jnp.ones_like(v)))
                total = m + jnp.log(o)
                hi = total.astype(bf16).astype(f32)
                rest = total - hi
                mid = rest.astype(bf16).astype(f32)
                aug = jnp.where(
                    lane == base,
                    hi,
                    jnp.where(lane == base + 1, mid, jnp.where(lane == base + 2, rest - mid, 0.0)),
                )
                qaug_ref[i, 2 * pair + a] = jnp.where(mine, q, aug.astype(bf16))
                outs.append(o * pl.reciprocal(pltpu.roll(o, HEAD_DIM, 1), approx=True))
            att_ref[:, cols] = jnp.where(low, outs[0], outs[1]).astype(bf16)


def attend_own_kernel(own, info, length, perm, x, w, b, att, qaug, kv, q_scr):
    attend_steps(own, info, length, perm, x, w, b, att, qaug, kv, q_scr)


def attend_other_kernel(own, info, length, perm, x, near, far, b, _, att, qaug, kv, w, q_scr):
    rows = near.shape[0]

    @pl.when(pl.program_id(0) == 0)
    def _():
        core = info[CORE]
        w[pl.ds(pl.multiple_of(core * rows, rows), rows), :] = near[...]
        w[pl.ds(pl.multiple_of((1 - core) * rows, rows), rows), :] = far[...]

    attend_steps(own, info, length, perm, x, w, b, att, qaug, kv, q_scr)


def attend(scalars, side, x, weights, biases, own, att=None):
    D = x.shape[1]
    half = D // 2
    heads = half // HEAD_DIM
    in_specs = [
        pl.BlockSpec((BLOCK, D), lambda s, n, *_: (block_row(jnp.minimum(s, own), n, own), 0)),
        *[whole(w.shape) for w in weights],
        whole(biases.shape),
    ]
    column = lambda n: n[HEAD] if side == 0 else 1 - n[HEAD]
    out_specs = [
        pl.BlockSpec((BLOCK, half), lambda s, n, *_: (jnp.maximum(s - own - 1, 0), column(n))),
        whole((own, heads, BLOCK, PAIR)),
        whole((own + 1, BLOCK, 2 * half)),
    ]
    out_shape = [
        jax.ShapeDtypeStruct((own * BLOCK, D), bf16),
        jax.ShapeDtypeStruct((own, heads, BLOCK, PAIR), bf16),
        jax.ShapeDtypeStruct((own + 1, BLOCK, 2 * half), bf16),
    ]
    operands = [*scalars, x, *weights, biases]
    aliases = {}
    if att is None:
        body = attend_own_kernel
    else:
        body = attend_other_kernel
        in_specs.append(pl.BlockSpec(memory_space=pl.ANY))
        operands.append(att)
        aliases = {len(operands) - 1: 0}
        out_specs.append(whole((D, 3 * half)))
        out_shape.append(jax.ShapeDtypeStruct((D, 3 * half), bf16))
    return pl.pallas_call(
        functools.partial(body, own),
        grid_spec=pltpu.PrefetchScalarGridSpec(
            num_scalar_prefetch=3,
            grid=(2 * own + 1,),
            in_specs=in_specs,
            out_specs=out_specs,
            scratch_shapes=[pltpu.VMEM((own, BLOCK, half), bf16)],
        ),
        out_shape=out_shape,
        input_output_aliases=aliases,
        compiler_params=params(),
        cost_estimate=QUICK,
        name="attend_forward",
    )(*operands)


def attend_back_kernel(
    own,
    info,
    length,
    perm,
    qaug_ref,
    kv_ref,
    att_ref,
    do_ref,
    x_ref,
    d_ref,
    near_ref,
    left_ref,
    right_ref,
    x_scr,
):
    step = pl.program_id(0)
    heads = qaug_ref.shape[1]
    half = heads * HEAD_DIM

    @pl.when(step == 0)
    def _():
        d_ref[...] = jnp.zeros_like(d_ref)

    x_scr[pl.ds(pl.multiple_of(step * BLOCK, BLOCK), BLOCK), :] = x_ref[...]

    @pl.when(step < own)
    def _():
        lane = lax.broadcasted_iota(jnp.int32, (BLOCK, PAIR), 1)
        low = lane < HEAD_DIM
        here = pl.ds(pl.multiple_of(step * BLOCK, BLOCK), BLOCK)
        for pair in range(heads // 2):
            cols = slice(pair * PAIR, pair * PAIR + PAIR)
            kcols = slice(half + pair * PAIR, half + pair * PAIR + PAIR)
            vcols = slice(2 * half + pair * PAIR, 2 * half + pair * PAIR + PAIR)
            do = do_ref[:, cols]
            prod = do.astype(f32) * att_ref[:, cols].astype(f32)
            dqs = []
            for a in range(2):
                c = key_place(own, info, length, perm, step, 2 * pair + a)
                mine = low if a == 0 else jnp.logical_not(low)
                base = HEAD_DIM if a == 0 else 0
                delta = jnp.sum(jnp.where(mine, prod, 0.0), axis=1, keepdims=True)
                hi = delta.astype(bf16).astype(f32)
                aug = jnp.where(lane == base, hi, jnp.where(lane == base + 1, delta - hi, 0.0))
                doaug = jnp.where(mine, do, aug.astype(bf16))
                k = kv_ref[c, :, cols]
                v = kv_ref[c, :, kcols]
                extra = jnp.where((lane >= base) & (lane < base + 3), -1.0, 0.0).astype(bf16)
                q = qaug_ref[0, 2 * pair + a]
                p = jnp.exp(dot(jnp.where(mine, k, extra), q, NT))
                ds = (p * dot(jnp.where(mine, v, extra), doaug, NT)).astype(bf16)
                dv = dot(p.astype(bf16), do).astype(bf16)
                dk = dot(ds, q).astype(bf16)
                dqs.append(dot(ds, k, TN) * SCALE)
                there = pl.ds(pl.multiple_of(c * BLOCK, BLOCK), BLOCK)
                d_ref[there, kcols] = jnp.where(mine, dk, d_ref[there, kcols])
                d_ref[there, vcols] = jnp.where(mine, dv, d_ref[there, vcols])
            d_ref[here, cols] = jnp.where(low, dqs[0], dqs[1]).astype(bf16)

    @pl.when(step == own)
    def _():
        core = info[CORE]
        d = d_ref[...]
        more = near_ref.shape[0] - half
        row = lax.broadcasted_iota(jnp.int32, (more, d.shape[1]), 0)
        sums = jnp.where(row == 0, colsum(d.astype(f32)), 0.0).astype(bf16)
        width = left_ref.shape[1]
        near_ref[half:, :] = sums
        left_ref[half:, :] = sums[:, :width]
        right_ref[half:, :] = sums[:, width:]
        x = x_scr[:, pl.ds(pl.multiple_of((1 - core) * half, half), half)]
        far = dot(x, d, TN).astype(bf16)
        left_ref[:half, :] = far[:, :width]
        right_ref[:half, :] = far[:, width:]
        x = x_scr[:, pl.ds(pl.multiple_of(core * half, half), half)]
        near_ref[:half, :] = dot(x, d, TN).astype(bf16)


def attend_back(scalars, side, qaug, kv, att, do, x, own):
    heads = qaug.shape[1]
    half = heads * HEAD_DIM
    D = x.shape[1]
    column = lambda n: n[HEAD] if side == 0 else 1 - n[HEAD]
    last = own - 1
    rows = pl.BlockSpec((BLOCK, half), lambda s, n, *_: (jnp.minimum(s, last), column(n)))
    d_shape = ((own + 1) * BLOCK, 3 * half)
    w_shape = (D // 2 + 16, 3 * half)
    w_parts = [(D // 2 + 16, width) for width in (2 * half - PAIR, half + PAIR)]
    return pl.pallas_call(
        functools.partial(attend_back_kernel, own),
        grid_spec=pltpu.PrefetchScalarGridSpec(
            num_scalar_prefetch=3,
            grid=(own + 1,),
            in_specs=[
                pl.BlockSpec(
                    (1, heads, BLOCK, PAIR), lambda s, *_: (jnp.minimum(s, last), 0, 0, 0)
                ),
                whole(kv.shape),
                rows,
                rows,
                pl.BlockSpec((BLOCK, D), lambda s, n, *_: (block_row(s, n, own), 0)),
            ],
            out_specs=[whole(d_shape), whole(w_shape), *[whole(w) for w in w_parts]],
            scratch_shapes=[pltpu.VMEM(((own + 1) * BLOCK, D), bf16)],
        ),
        out_shape=[
            jax.ShapeDtypeStruct(d_shape, bf16),
            jax.ShapeDtypeStruct(w_shape, bf16),
            *[jax.ShapeDtypeStruct(w, bf16) for w in w_parts],
        ],
        compiler_params=params(),
        cost_estimate=QUICK,
        name="attend_backward",
    )(*scalars, qaug, kv, att, do, x)


def norm_terms(z):
    mean = jnp.mean(z, axis=1, keepdims=True)
    centred = z - mean
    variance = jnp.mean(centred * centred, axis=1, keepdims=True)
    inverse = lax.rsqrt(variance + EPS)
    return centred * inverse, inverse


def norm_back(incoming, normed, inverse, gain):
    scaled = incoming * gain
    first = jnp.mean(scaled, axis=1, keepdims=True)
    second = jnp.mean(scaled * normed, axis=1, keepdims=True)
    return inverse * (scaled - first - normed * second)


def gelu_parts(v):
    cdf = 0.5 + 0.5 * lax.erf(v * math.sqrt(0.5))
    return v * cdf, cdf + v * (math.sqrt(0.5 / math.pi) * jnp.exp(v * (v * -0.5)))


def add_up(acc, rows, cols, value):
    first = pl.program_id(0) == 0
    acc[rows, cols] = jnp.where(first, value, value + acc[rows, cols])


OUT_ROWS = 32


def place_piece(info, c, y, x, near_ref, far_ref, rows, cols, piece):
    number = (info[HEAD] ^ y) * 2 + (info[NEXT] ^ x)

    @pl.when(info[CORE] == c)
    def _():
        near_ref[number, rows, cols] = piece

    @pl.when(info[CORE] != c)
    def _():
        far_ref[number, rows, cols] = piece


def middle_up_kernel(
    info,
    att_ref,
    x_ref,
    cot_ref,
    c_ref,
    wo_ref,
    wu_ref,
    wd_ref,
    out_ref,
    slope_ref,
    n1_ref,
    inv_ref,
    gsec_ref,
    near_ref,
    far_ref,
    vec_ref,
    act_scr,
    acc,
):
    i = pl.program_id(0)
    D, ff = wu_ref.shape
    bo, g1, s1, bd, g2, s2 = (c_ref[r : r + 1, :] for r in range(6))
    branch = dot(att_ref[...], wo_ref[...]) + bo
    n1, inv1 = norm_terms(x_ref[...].astype(f32) + branch)
    n1_ref[...] = n1
    inv_ref[...] = jnp.broadcast_to(inv1, inv_ref.shape)
    y1 = n1 * g1 + s1
    upin = y1.astype(bf16)
    ffn = bd
    for f in range(ff // D):
        cols = slice(f * D, f * D + D)
        value, slope = gelu_parts(dot(upin, wu_ref[:, cols]) + c_ref[8 + f : 9 + f, :])
        act = value.astype(bf16)
        act_scr[:, cols] = act
        slope_ref[:, cols] = slope.astype(bf16)
        ffn = ffn + dot(act, wd_ref[cols, :])
    n2, inv2 = norm_terms(y1 + ffn)
    out_ref[...] = (n2 * g2 + s2).astype(bf16)
    e = cot_ref[...].astype(f32)
    gsec = norm_back(e, n2, inv2, g2)
    gsec_ref[...] = gsec
    gffn = gsec.astype(bf16)
    for f in range(ff // D):
        cols = slice(f * D, f * D + D)
        add_up(acc, cols, slice(None), dot(act_scr[:, cols], gffn, TN))

    @pl.when(i == 0)
    def _():
        vec_ref[...] = jnp.zeros_like(vec_ref)

    for row, values in ((3, gffn.astype(f32)), (4, e * n2), (5, e)):
        vec_ref[row : row + 1, :] += colsum(values)

    @pl.when(i == pl.num_programs(0) - 1)
    def _():
        half = D // 2
        for f in range(ff // D):
            for y in range(2):
                piece = acc[f * D : f * D + D, y * half : y * half + half].astype(bf16)
                place_piece(
                    info, f // 2, y, f % 2, near_ref, far_ref, slice(None), slice(None), piece
                )


def middle_up(info, att, x, cot, wo, wu, wd, consts, tile=BLOCK // 2):
    R, D = att.shape
    FF = wu.shape[1]
    tiles = R // tile
    row = lambda width: pl.BlockSpec((tile, width), lambda s, n: (s, 0))
    kept = pl.BlockSpec(memory_space=pltpu.VMEM)
    sd = jax.ShapeDtypeStruct
    pieces = (4, FF // 4, D // 2)
    return pl.pallas_call(
        middle_up_kernel,
        grid_spec=pltpu.PrefetchScalarGridSpec(
            num_scalar_prefetch=1,
            grid=(tiles,),
            in_specs=[
                row(D),
                pl.BlockSpec((tile, D), lambda s, n: (s + n[HEAD] * tiles, 0)),
                row(D),
                whole(consts.shape),
                kept,
                kept,
                kept,
            ],
            out_specs=[row(D), row(FF), row(D), row(128), row(D)]
            + [whole(pieces), whole(pieces), whole(consts.shape)],
            scratch_shapes=[
                pltpu.VMEM((tile, FF), bf16),
                pltpu.VMEM((FF, D), f32),
            ],
        ),
        out_shape=[
            sd((R, D), bf16),
            sd((R, FF), bf16),
            sd((R, D), f32),
            sd((R, 128), f32),
            sd((R, D), f32),
            sd(pieces, bf16),
            sd(pieces, bf16),
            sd(consts.shape, f32),
        ],
        compiler_params=params(44),
        cost_estimate=QUICK,
        name="middle_up",
    )(info, att, x, cot, consts, wo, wu, wd)


def middle_down_kernel(
    info,
    att_ref,
    slope_ref,
    n1_ref,
    inv_ref,
    gsec_ref,
    vec_in_ref,
    c_ref,
    wo_ref,
    wu_ref,
    wd_ref,
    gatt_ref,
    gfirst_ref,
    near_ref,
    far_ref,
    vec_ref,
    gp_scr,
    acc,
    acc_out,
):
    i = pl.program_id(0)
    D, ff = wu_ref.shape

    @pl.when(i == 0)
    def _():
        vec_ref[...] = vec_in_ref[...]

    g1, s1 = c_ref[1:2, :], c_ref[2:3, :]
    n1 = n1_ref[...]
    upin = (n1 * g1 + s1).astype(bf16)
    gsec = gsec_ref[...]
    gffn = gsec.astype(bf16)
    for f in range(ff // D):
        cols = slice(f * D, f * D + D)
        gp = (dot(gffn, wd_ref[cols, :], NT) * slope_ref[:, cols].astype(f32)).astype(bf16)
        gp_scr[:, cols] = gp
        vec_ref[8 + f : 9 + f, :] += colsum(gp.astype(f32))
    gnormed = gsec
    for f in range(ff // D):
        cols = slice(f * D, f * D + D)
        gp = gp_scr[:, cols]
        gnormed = gnormed + dot(gp, wu_ref[:, cols], NT)
        add_up(acc, slice(None), cols, dot(upin, gp, TN))
    gfirst = norm_back(gnormed, n1, inv_ref[:, :1], g1)
    gfirst_ref[...] = gfirst
    gbr = gfirst.astype(bf16)
    gatt_ref[...] = dot(gbr, wo_ref[...], NT).astype(bf16)
    add_up(acc_out, slice(None), slice(None), dot(gbr, att_ref[...], TN))
    for row, values in enumerate((gbr.astype(f32), gnormed * n1, gnormed)):
        vec_ref[row : row + 1, :] += colsum(values)

    @pl.when(i == pl.num_programs(0) - 1)
    def _():
        half, few = D // 2, D // 32
        for f in range(ff // D):
            for x in range(2):
                piece = acc[x * half : x * half + half, f * D : f * D + D].astype(bf16)
                place_piece(
                    info, f % 2, f // 2, x, near_ref, far_ref, slice(0, half), slice(None), piece
                )
        sums = vec_ref[...].astype(bf16)
        for number in range(4):
            near_ref[number, half + 4 * OUT_ROWS :, :] = sums
            far_ref[number, half + 4 * OUT_ROWS :, :] = sums
        for c in range(2):
            for y in range(2):
                for x in range(2):
                    for q in range(4):
                        top = (8 * y + 4 * x + q) * 2 * few
                        both = acc_out[top : top + 2 * few, c * half : c * half + half]
                        both = jnp.concatenate([both[:few], both[few:]], axis=1)
                        pad = jnp.zeros((OUT_ROWS - few, D), f32)
                        both = jnp.concatenate([both, pad], axis=0).astype(bf16)
                        rows = slice(half + q * OUT_ROWS, half + q * OUT_ROWS + OUT_ROWS)
                        place_piece(info, c, y, x, near_ref, far_ref, rows, slice(None), both)


def middle_down(info, att, saved, vectors, wo, wu, wd, consts, tile=BLOCK // 2):
    R, D = att.shape
    FF = wu.shape[1]
    row = lambda width: pl.BlockSpec((tile, width), lambda s, n: (s, 0))
    kept = pl.BlockSpec(memory_space=pltpu.VMEM)
    sd = jax.ShapeDtypeStruct
    pieces = (4, D // 2 + 4 * OUT_ROWS + consts.shape[0], FF // 4)
    return pl.pallas_call(
        middle_down_kernel,
        grid_spec=pltpu.PrefetchScalarGridSpec(
            num_scalar_prefetch=1,
            grid=(R // tile,),
            in_specs=[row(D), row(FF), row(D), row(128), row(D)]
            + [whole(consts.shape)] * 2
            + [kept] * 3,
            out_specs=[row(D), row(D), whole(pieces), whole(pieces)],
            scratch_shapes=[
                pltpu.VMEM(consts.shape, f32),
                pltpu.VMEM((tile, FF), bf16),
                pltpu.VMEM((D, FF), f32),
                pltpu.VMEM((D, D), f32),
            ],
        ),
        out_shape=[
            sd((R, D), bf16),
            sd((R, D), f32),
            sd(pieces, bf16),
            sd(pieces, bf16),
        ],
        compiler_params=params(44),
        cost_estimate=QUICK,
        name="middle_down",
    )(info, att, *saved, vectors, consts, wo, wu, wd)


def input_kernel(own, info, da, db, wa, wb, first, out_ref, next_ref):
    total = dot(da[...], wa[...], NT) + dot(db[...], wb[...], NT)

    @pl.when(pl.program_id(0) == 0)
    def _():
        next_ref[...] = total.astype(bf16)

    @pl.when(pl.program_id(0) > 0)
    def _():
        out_ref[...] = total + first[...]


def input_call(info, da, db, wa, wb, first, own):
    D, width = wa.shape
    row = pl.BlockSpec((BLOCK, width), lambda s, n: (jnp.where(s == 0, own, s - 1), 0))
    wide = pl.BlockSpec((BLOCK, D), lambda s, n: (jnp.maximum(s - 1, 0), 0))
    return pl.pallas_call(
        functools.partial(input_kernel, own),
        grid_spec=pltpu.PrefetchScalarGridSpec(
            num_scalar_prefetch=1,
            grid=(own + 1,),
            in_specs=[row, row, whole((D, width)), whole((D, width)), wide],
            out_specs=[wide, whole((BLOCK, D))],
        ),
        out_shape=[
            jax.ShapeDtypeStruct(first.shape, f32),
            jax.ShapeDtypeStruct((BLOCK, D), bf16),
        ],
        compiler_params=params(60),
        cost_estimate=QUICK,
        name="input_grad",
    )(info, da, db, wa, wb, first)


def edge_kernel(info, recv, rest, out_ref):
    out_ref[...] = rest[...] + recv[...].astype(f32)


def edge_call(info, recv, rest, own):
    D = rest.shape[1]
    edge = pl.BlockSpec((BLOCK // 4, D), lambda s, n: (s + 4 * jnp.where(n[HEAD] == 0, own - 1, 0), 0))
    return pl.pallas_call(
        edge_kernel,
        grid_spec=pltpu.PrefetchScalarGridSpec(
            num_scalar_prefetch=1,
            grid=(4,),
            in_specs=[pl.BlockSpec((BLOCK // 4, D), lambda s, n: (s, 0)), edge],
            out_specs=edge,
        ),
        out_shape=jax.ShapeDtypeStruct(rest.shape, f32),
        input_output_aliases={2: 0},
        compiler_params=params(),
        cost_estimate=QUICK,
        name="edge_block",
    )(info, recv, rest)


def finish_up_kernel(info, vec_in_ref, parts, *refs):
    up_ref, out_ref, sums_ref, *vec_refs, scr = refs
    width = parts.shape[2]
    half, few = width // 2, width // 32
    count = parts.shape[0] // 4
    rows, size = half // count, parts.shape[1]
    for c in range(2):
        for x in range(2):
            for q in range(count):
                piece = parts[(2 * c + x) * count + q].astype(f32)
                up_ref[
                    x * half + q * rows : x * half + q * rows + rows, c * width : c * width + width
                ] = piece[:rows]
                for n in range(2):
                    top = x * (half // 2) + (2 * q + n) * few
                    scr[top : top + few, c * half : c * half + half] = piece[
                        rows : rows + few, n * half : n * half + half
                    ]
    out_ref[...] = scr[...].T
    vectors = vec_in_ref[...].astype(f32)
    mine = jnp.where(info[HEAD] == 0, vectors[:, :half], vectors[:, half:])
    for row, ref in enumerate(vec_refs):
        ref[...] = mine[row]
    chunks = sums_ref.shape[0] // width
    for n in range(chunks):
        both = jnp.where(info[HEAD] == 0, vectors[8 + n], vectors[8 + chunks + n])
        sums_ref[n * width : n * width + width] = both


def finish_up(info, vectors, parts):
    width = parts.shape[2]
    outs = [
        ((width, 2 * width), f32),
        ((width, width // 2), f32),
        ((2 * width,), f32),
        *[((width // 2,), f32)] * 6,
    ]
    scratch = [pltpu.VMEM((width // 2, width), f32)]
    return small_call(finish_up_kernel, "finish_up", outs, [info], [vectors, parts], scratch, True)


def small_call(kernel, name, outs, scalars, arrays, scratch=(), whole_arrays=False, mib=40):
    smem = pl.BlockSpec(memory_space=pltpu.SMEM)

    def spec(array):
        if array.ndim < 3 or whole_arrays:
            return whole(array.shape)
        shape = (None, *array.shape[1:])
        return pl.BlockSpec(shape, lambda _: (0, 0, 0), pipeline_mode=pl.Buffered(1))

    return pl.pallas_call(
        kernel,
        grid=(1,),
        in_specs=[smem] * len(scalars) + [spec(array) for array in arrays],
        out_specs=[whole(shape) for shape, _ in outs],
        out_shape=[jax.ShapeDtypeStruct(shape, kind) for shape, kind in outs],
        scratch_shapes=list(scratch),
        compiler_params=params(mib),
        cost_estimate=QUICK,
        name=name,
    )(*scalars, *arrays)


def quarters_kernel(sections, at, place, *refs):
    terms, outs = refs[:-4], refs[-4:]
    for n, out in enumerate(outs):
        done = 0
        parts = [(start + (place[at] ^ n) * (rows // 4), rows // 4) for start, rows in sections]
        for top, rows in parts + [(sum(sections[-1]), 16)]:
            if not isinstance(top, int):
                top = pl.multiple_of(top, 16)
            values = [term[pl.ds(top, rows), :].astype(f32) for term in terms]
            if values[-1].shape[1] < out.shape[1]:
                values[-2:] = [jnp.concatenate(values[-2:], axis=1)]
            out[done : done + rows, :] = sum(values).astype(out.dtype)
            done += rows


def quarters(sections, at, place, terms):
    rows, width = sum(rows // 4 for _, rows in sections) + 16, terms[0].shape[1]
    outs = [((rows, width), f32)] + [((rows, width), bf16)] * 3
    kernel = functools.partial(quarters_kernel, sections, at)
    return small_call(kernel, "quarters", outs, [place], terms, mib=60)


def join_cores_kernel(near, left, right, out):
    far = jnp.concatenate([left[...].astype(f32), right[...].astype(f32)], axis=1)
    out[...] = (near[...].astype(f32) + far).astype(bf16)


def join_cores(near, left, right):
    outs = [(near.shape, bf16)]
    return small_call(join_cores_kernel, "join_cores", outs, [], [near, left, right])[0]


def settle_up_kernel(*refs):
    terms, (part, vectors) = refs[:-2], refs[-2:]
    rows = part.shape[0]
    part[...] = sum(term[:rows, :].astype(f32) for term in terms).astype(bf16)
    vectors[...] = sum(term[rows:, :].astype(f32) for term in terms)


def settle_up(terms):
    rows, width = terms[0].shape
    outs = [((rows - 16, width), bf16), ((16, width), f32)]
    return small_call(settle_up_kernel, "settle_up", outs, [], terms)


def add_up_kernel(*refs):
    terms, (kept, sent) = refs[:4], refs[4:]
    total = sum(term[...].astype(f32) for term in terms)
    kept[...] = total
    sent[...] = total.astype(bf16)


def add_all(terms):
    shape = terms[0].shape
    return small_call(add_up_kernel, "add_all", [(shape, f32), (shape, bf16)], [], terms)


def settle_kernel(kept, got, part, q_sum, v_sum):
    few, width = part.shape
    half = width // 3
    total = kept[...] + got[...].astype(f32)
    part[...] = total[:few].astype(bf16)
    q_sum[...] = total[few, :half]
    v_sum[...] = total[few, 2 * half :]


def settle(kept, got):
    rows, width = kept.shape
    outs = [((rows - 16, width), bf16), ((width // 3,), f32), ((width // 3,), f32)]
    return small_call(settle_kernel, "settle", outs, [], [kept, got])


def finish_qkv_kernel(info, place, *refs):
    pieces, outs = refs[:8], refs[8:]
    rows = pieces[0].shape[0]
    half = outs[0].shape[1]
    for n, ref in enumerate(pieces):
        core = info[CORE] ^ (n // 4)
        top = pl.multiple_of((4 * core + (place[0] ^ (n % 4))) * rows, 8)
        piece = ref[...].astype(f32)
        for m, out in enumerate(outs):
            out[pl.ds(top, rows), :] = piece[:, m * half : m * half + half]


def finish_qkv(info, place, pieces):
    rows, width = pieces[0].shape
    outs = [((8 * rows, width // 3), f32)] * 3
    return small_call(finish_qkv_kernel, "finish_qkv", outs, [info, place], pieces)


def flip_head(value):
    return lax.ppermute(value, "head", [(0, 1), (1, 0)])


def flip_dp(value, bit):
    size = lax.axis_size("dp")
    return lax.ppermute(value, "dp", [(i, i ^ (1 << bit)) for i in range(size)])


def flip_both(value, bit):
    size = lax.axis_size("dp")
    pairs = [(2 * i + h, 2 * (i ^ (1 << bit)) + 1 - h) for i in range(size) for h in range(2)]
    return lax.ppermute(value, ("dp", "head"), pairs)


def bit_of(bit):
    return (lax.axis_index("dp") >> bit) & 1


def dp_bits(first):
    return list(range(first, (lax.axis_size("dp") - 1).bit_length()))


def flip_quarter(value, number, bit):
    size = lax.axis_size("dp")
    return lax.ppermute(value, "dp", [(i, i ^ (number << bit)) for i in range(size)])


def total_of(terms):
    total = 0.0
    for term in terms:
        total = total + term.astype(f32)
    return total.astype(bf16)


def rows_of(terms, place, rows):
    return total_of([lax.dynamic_slice_in_dim(term, place * rows, rows, 0) for term in terms])


def gather_pieces(part):
    size = lax.axis_size("dp")
    one = [c + 2 * x + 4 * q for c in range(2) for x in range(2) for q in range(4)]
    groups = [[16 * k + i for i in one] for k in range(size // 16)]
    return lax.all_gather(part, "dp", axis_index_groups=groups)


def scatter_rest(part):
    size = lax.axis_size("dp")
    groups = [[i + 4 * k for k in range(size // 4)] for i in range(4)]
    return lax.psum_scatter(part, "dp", axis_index_groups=groups, tiled=True)


def gather_all(part):
    size = lax.axis_size("dp")
    group = [c + 2 * x + 4 * k for c in range(2) for x in range(2) for k in range(size // 4)]
    return lax.all_gather(part, "dp", axis_index_groups=[group])


def finish_quarters(kept, got):
    part, sums = settle_up([kept, *got])
    for bit in dp_bits(4):
        size = part.shape[0] // 2
        part_got = flip_dp(rows_of([part], 1 - bit_of(bit), size), bit)
        part = total_of([rows_of([part], bit_of(bit), size), part_got])
        sums = sums + flip_dp(sums, bit)
    for bit in dp_bits(4)[::-1]:
        part = join(part, flip_dp(part, bit), bit_of(bit), 0)
    return part, sums


def order(*values):
    return lax.optimization_barrier(values)


def join(mine, theirs, own, axis):
    first = jnp.where(own == 0, mine, theirs)
    second = jnp.where(own == 0, theirs, mine)
    return jnp.concatenate([first, second], axis=axis)


def body(
    hidden_in,
    w_query,
    b_query,
    w_key,
    w_value,
    b_value,
    w_out,
    b_out,
    gain_one,
    shift_one,
    w_up,
    b_up,
    w_down,
    b_down,
    gain_two,
    shift_two,
    seq_length,
    block_perm,
    cotangent,
):
    D, half = w_query.shape
    FF = w_up.shape[1]
    own = hidden_in.shape[0] // BLOCK // 2
    head = lax.axis_index("head")
    core = bit_of(0)
    mine = (w_query, w_key, w_value)

    rows = D // 2
    near = flip_head(
        jnp.concatenate([lax.dynamic_slice_in_dim(w, core * rows, rows, 0) for w in mine], 1)
    )
    w_a = jnp.concatenate(mine, 1)
    bias_a = jnp.stack([b_query, b_value])
    bias_b = flip_head(bias_a)
    perm_b = flip_head(block_perm)
    place = lax.broadcasted_iota(jnp.int32, (3,), 0)
    info = jnp.where(place == HEAD, head, jnp.where(place == CORE, core, bit_of(1))).astype(
        jnp.int32
    )
    scalars_a = (info, seq_length, block_perm)
    scalars_b = (info, seq_length, perm_b)
    zeros = jnp.zeros((D,), f32)
    consts = jnp.concatenate(
        [
            jnp.stack([b_out, gain_one, shift_one, b_down, gain_two, shift_two, zeros, zeros]),
            b_up.reshape(FF // D, D),
            jnp.zeros((8 - FF // D, D), f32),
        ]
    )

    att, q_a, kv_a = attend(scalars_a, 0, hidden_in, (w_a,), bias_a, own)
    near, att = order(near, att)
    far = flip_dp(near, 0)
    att, q_b, kv_b, w_b = attend(scalars_b, 1, hidden_in, (near, far), bias_b, own, att)

    dp = lax.axis_index("dp")
    slot = lax.broadcasted_iota(jnp.int32, (3,), 0)
    place = jnp.where(slot == 0, (dp >> 1) & 3, jnp.where(slot == 1, (dp >> 3) & 1, (dp >> 2) & 3))
    place = place.astype(jnp.int32)

    block_out, *saved, down_near, down_far, vectors = middle_up(
        info, att, hidden_in, cotangent, w_out, w_up, w_down, consts
    )
    down_far = flip_dp(down_far, 0)

    def leave(mine, sent):
        return [total_of([mine[n], sent[n]]) for n in (1, 2, 3)]

    def across(beside, over, corner):
        return [flip_both(corner, 1), flip_head(over), flip_dp(beside, 1)]

    att, *leaving = order(att, *leave(down_near, down_far))
    down = across(*leaving)
    gatt, gfirst, up_near, up_far = middle_down(
        info, att, saved, vectors, w_out, w_up, w_down, consts
    )
    gatt, up_far, *down = order(gatt, up_far, *down)
    up_far = flip_dp(up_far, 0)
    down = total_of([*down, down_near[0], down_far[0]])
    up_far, down = order(up_far, down)
    down = scatter_rest(down)
    gatt, *up = order(gatt, *leave(up_near, up_far))
    up = across(*up)
    d_b, near_b, *far_b = attend_back(scalars_b, 1, q_b, kv_b, att, gatt, hidden_in, own)
    d_b, down, *more = order(d_b, down, *up, *far_b)
    up, far_b = more[:3], [flip_dp(far, 0) for far in more[3:]]
    sections = ((0, D // 2), (D // 2, 4 * OUT_ROWS))
    up_kept, *up = quarters(sections, 2, place, [*up, up_near, up_far])
    gatt, near_b, *up = order(gatt, join_cores(near_b, *far_b), *up)
    from_other = flip_head(near_b)
    up = [flip_quarter(value, n + 1, 2) for n, value in enumerate(up)]
    down = gather_all(down)
    d_a, near_a, *far_a = attend_back(scalars_a, 0, q_a, kv_a, att, gatt, hidden_in, own)

    from_other, d_a, *more = order(from_other, d_a, *up, *far_a)
    up, far_a = more[:3], [flip_dp(far, 0) for far in more[3:]]
    up, vectors = finish_quarters(up_kept, up)
    up = gather_pieces(up)

    kept, *out = quarters(((0, rows),), 0, place, [near_a, from_other, *far_a])
    d_a, *out = order(d_a, *out)
    got = [flip_quarter(value, n + 1, 1) for n, value in enumerate(out)]
    input_grad, next_block = input_call(info, d_a, d_b, w_a, w_b, gfirst, own)
    input_grad, *got = order(input_grad, *got)
    kept, sent = add_all([kept, *got])
    next_block, sent = order(next_block, sent)
    recv = flip_head(next_block)
    part, sum_q, sum_v = settle(kept, flip_dp(sent, 3))
    for bit in dp_bits(4):
        size = part.shape[0] // 2
        part_got = flip_dp(rows_of([part], 1 - bit_of(bit), size), bit)
        part = total_of([rows_of([part], bit_of(bit), size), part_got])
        sum_q, sum_v = sum_q + flip_dp(sum_q, bit), sum_v + flip_dp(sum_v, bit)
    for bit in dp_bits(4)[::-1]:
        part = join(part, flip_dp(part, bit), bit_of(bit), 0)
    part, down = order(part, down)
    got = [flip_quarter(part, n, 1) for n in (1, 2, 3)]
    grad_down = down.reshape(FF, half).astype(f32)
    input_grad = edge_call(info, recv, input_grad, own)
    grad_down, input_grad, *got = order(grad_down, input_grad, *got)
    pieces = [part, *got]
    pieces += [flip_dp(piece, 0) for piece in pieces]
    grad_q, grad_k, grad_v = finish_qkv(info, place, pieces)
    grad_q, up, vectors = order(grad_q, up, vectors)
    grad_up, grad_out, sum_up, *sums = finish_up(info, vectors, up)
    return (
        block_out,
        input_grad,
        grad_q,
        sum_q,
        grad_k,
        grad_v,
        sum_v,
        grad_out,
        sums[0],
        sums[1],
        sums[2],
        grad_up,
        sum_up,
        grad_down,
        sums[3],
        sums[4],
        sums[5],
    )


def solution(mesh):
    rows = P(("dp", "head"), None)
    cols = P(None, "head")
    piece = P("head")
    return jax.shard_map(
        body,
        mesh=mesh,
        in_specs=(
            P("dp", None),
            cols,
            piece,
            cols,
            cols,
            piece,
            *[P()] * 10,
            P("dp"),
            P("dp", "head"),
            rows,
        ),
        out_specs=(
            rows,
            rows,
            cols,
            piece,
            cols,
            cols,
            piece,
            cols,
            piece,
            piece,
            piece,
            cols,
            piece,
            cols,
            piece,
            piece,
            piece,
        ),
        check_vma=False,
    )
```
